256 devices in a mesh: section: 8 (over x_hi, y), expert: 32 (over z, x_lo, core).
Axes of the slice: x: 4 (x_hi: 2, x_lo: 2; x = x_hi * 2 + x_lo), y: 4, z: 8, core: 2. Of those that a mesh axis runs over, the one named last changes fastest.
Arguments:
- acts: bfloat16 [8, 8192, 2048], P('section', 'expert'), may hold values from -6 to 6
- grad_out: bfloat16 [8, 8192, 2048], P('section', 'expert'), may hold values from -6 to 6
- expert_of: int32 [8, 8192, 2], P('section', 'expert'), may hold values from 0 to 31, as said below
- slot_of: int32 [8, 8192, 2], P('section', 'expert'), may hold values from 0 to 1023, as said below
- source_row: int32 [8, 32, 1024], P('section', None, 'expert'), may hold values from -1 to 8191, as said below
- combine: bfloat16 [8, 8192, 2], P('section', 'expert'), may hold values from 0.099609375 to 1
- w_gate: bfloat16 [8, 32, 2048, 384], P('section', 'expert'), may hold values from -0.125 to 0.125
- w_up: bfloat16 [8, 32, 2048, 384], P('section', 'expert'), may hold values from -0.125 to 0.125
- w_down: bfloat16 [8, 32, 384, 2048], P('section', 'expert'), may hold values from -0.3125 to 0.3125
Outputs:
- grad_acts: bfloat16 [8, 8192, 2048], P('section', 'expert')
- grad_combine: bfloat16 [8, 8192, 2], P('section', 'expert')
- grad_gate: bfloat16 [8, 32, 2048, 384], P('section', 'expert')
- grad_up: bfloat16 [8, 32, 2048, 384], P('section', 'expert')
- grad_down: bfloat16 [8, 32, 384, 2048], P('section', 'expert')
The draws below stay inside these ranges and needn't reach their ends.
Inputs may be any that keep to these rules, and one draw needn't show every extreme that they name: `expert_of`: each token names 2 different experts. Within the rows of one index of expert, no expert is named more than 32 times, and some expert exactly 32 times. `slot_of`: A token of the j-th block of 256 rows of a section takes a slot c of its expert with c // 32 = j; no two tokens share a slot; in every block some expert uses all 32 slots of that block. `source_row`: exactly the inverse of expert_of and slot_of: slot c of expert e holds the token that names e with slot c, or -1 where none does.
All inputs are finite; a program needn't handle non-finite values.
Results may differ from the reference program's by a relative error of at most 0.0065.
Values may be sent and summed in bfloat16 or wider, within the bound.
No kernel may reach another device: no remote copies, remote signals or barrier semaphores. Data moves between devices by JAX's collectives and lax.ppermute only.
A program may use at most 128 MiB of HBM per device.

```python
import jax
import jax.numpy as jnp
from jax import lax

D = 2048
FF = 384
TOP = 2
TOK_DEV = 256
SECTIONS = 8
EXPERTS = 32
TOKENS = 8192
MOST = 32
CAP = 1024


def route_tables(key):
    key_target, key_order, key_offset, key_rows = jax.random.split(key, 4)
    block_count = SECTIONS * EXPERTS
    half_count = EXPERTS // 2
    middle = MOST // 2
    expert_range = jnp.arange(EXPERTS, dtype=jnp.int32)
    target = jnp.repeat(jax.random.randint(key_target, (SECTIONS,), 0, EXPERTS), EXPERTS)
    order_scores = jax.random.randint(key_order, (block_count, EXPERTS), 0, 1 << 20) * EXPERTS + expert_range[None, :]
    order_scores = jnp.where(expert_range[None, :] == target[:, None], -1, order_scores)
    order = jnp.argsort(order_scores, axis=1).astype(jnp.int32)
    offsets = jax.random.randint(key_offset, (block_count, half_count), 0, middle + 1)
    offsets = offsets.at[:, 0].set(middle)
    paired = jnp.concatenate([middle + offsets, middle - offsets], axis=1).astype(jnp.int32)
    block_range = jnp.arange(block_count, dtype=jnp.int32)
    counts = jnp.zeros((block_count, EXPERTS), jnp.int32).at[block_range[:, None], order].set(paired)
    ends = jnp.cumsum(counts, axis=1)
    starts = ends - counts
    positions = jnp.arange(TOK_DEV * TOP, dtype=jnp.int32)
    seq_expert = jnp.sum((ends[:, None, :] <= positions[None, :, None]).astype(jnp.int32), axis=2)
    seq_rank = positions[None, :] - jnp.take_along_axis(starts, seq_expert, axis=1)
    row_keys = jax.random.split(key_rows, block_count)
    row_order = jax.vmap(lambda row_key: jax.random.permutation(row_key, TOK_DEV))(row_keys).astype(jnp.int32)
    inverse = jnp.argsort(row_order, axis=1).astype(jnp.int32)
    pos_index = (inverse[:, :, None] + TOK_DEV * jnp.arange(TOP, dtype=jnp.int32)[None, None, :]).reshape(block_count, TOK_DEV * TOP)
    source_block = block_range % EXPERTS
    expert_table = jnp.take_along_axis(seq_expert, pos_index, axis=1).reshape(SECTIONS, TOKENS, TOP)
    rank_table = jnp.take_along_axis(seq_rank, pos_index, axis=1).reshape(block_count, TOK_DEV, TOP)
    slot_table = (rank_table + source_block[:, None, None] * MOST).reshape(SECTIONS, TOKENS, TOP)
    slot_rank = jnp.arange(MOST, dtype=jnp.int32)
    seq_pos = starts[:, :, None] + slot_rank[None, None, :]
    filled = slot_rank[None, None, :] < counts[:, :, None]
    row_local = jnp.take_along_axis(row_order, (seq_pos % TOK_DEV).reshape(block_count, EXPERTS * MOST), axis=1)
    row_local = row_local.reshape(block_count, EXPERTS, MOST)
    source_table = jnp.where(filled, source_block[:, None, None] * TOK_DEV + row_local, -1)
    source_table = source_table.reshape(SECTIONS, EXPERTS, EXPERTS, MOST).transpose(0, 2, 1, 3).reshape(SECTIONS, EXPERTS, CAP)
    return (expert_table.astype(jnp.int32), slot_table.astype(jnp.int32), source_table.astype(jnp.int32))


def draw_expert_of(key, part):
    return route_tables(key)[0]


def draw_slot_of(key, part):
    return route_tables(key)[1]


def draw_source_row(key, part):
    return route_tables(key)[2]


def level_of(stream_key, dims, cuts, least, largest):
    level, own = 1.0, jax.random.fold_in(stream_key, 6)
    for axis_at, shards_of in cuts:
        heights = jnp.exp(jax.random.uniform(jax.random.fold_in(own, axis_at), (shards_of,), jnp.float32, least / len(cuts), largest / len(cuts)))
        level = level * jnp.repeat(heights, dims[axis_at] // shards_of).reshape([-1 if axis == axis_at else 1 for axis in range(len(dims))])
    return level


def noise(key, dims, deviation, bound, cuts=(), kind=jnp.bfloat16):
    result = deviation * jax.random.normal(key, dims, jnp.float32)
    if cuts:
        result = result * level_of(key, dims, cuts, -0.22, 0.18)
    return jnp.clip(result, -bound, bound).astype(kind)


def setup_inputs(seed: int = 0) -> dict:
    key_of = jax.random.split(jax.random.key(seed), 10)
    return {
        "acts": noise(key_of[0], (SECTIONS, TOKENS, D), 1.0, 6.0, ((0, 8), (1, 32))),
        "grad_out": noise(key_of[1], (SECTIONS, TOKENS, D), 1.0, 6.0, ((0, 8), (1, 32))),
        "expert_of": draw_expert_of(jax.random.fold_in(key_of[9], 71), 0),
        "slot_of": draw_slot_of(jax.random.fold_in(key_of[9], 71), 0),
        "source_row": draw_source_row(jax.random.fold_in(key_of[9], 71), 0),
        "combine": jnp.clip(0.099609375 + 0.9003906 * jax.random.uniform(key_of[5], (SECTIONS, TOKENS, TOP), jnp.float32) ** level_of(key_of[5], (SECTIONS, TOKENS, TOP), ((0, 8), (1, 32)), -0.2, 0.2), 0.099609375, 1.0).astype(jnp.bfloat16),
        "w_gate": noise(key_of[6], (SECTIONS, EXPERTS, D, FF), D ** -0.5, 0.125, ((0, 8), (1, 32))),
        "w_up": noise(key_of[7], (SECTIONS, EXPERTS, D, FF), D ** -0.5, 0.125, ((0, 8), (1, 32))),
        "w_down": noise(key_of[8], (SECTIONS, EXPERTS, FF, D), FF ** -0.5, 0.3125, ((0, 8), (1, 32))),
    }


def forward_rows(x_rows, weight_gate, weight_up, weight_down):
    pre_gate = jnp.dot(x_rows, weight_gate, preferred_element_type=jnp.float32)
    pre_up = jnp.dot(x_rows, weight_up, preferred_element_type=jnp.float32)
    sigmoid_gate = jax.nn.sigmoid(pre_gate)
    silu_gate = pre_gate * sigmoid_gate
    hidden = (silu_gate * pre_up).astype(jnp.bfloat16)
    expert_out = jnp.dot(hidden, weight_down, preferred_element_type=jnp.float32)
    return pre_gate, pre_up, sigmoid_gate, silu_gate, hidden, expert_out


def backward_rows(x_rows, g_rows, slot_weight, state, weight_gate, weight_up, weight_down):
    pre_gate, pre_up, sigmoid_gate, silu_gate, hidden, expert_out = state
    slot_score = jnp.sum(expert_out * g_rows.astype(jnp.float32), axis=1).astype(jnp.bfloat16)
    scaled = (slot_weight.astype(jnp.float32)[:, None] * g_rows.astype(jnp.float32)).astype(jnp.bfloat16)
    first = (((0,), (0,)), ((), ()))
    second = (((1,), (1,)), ((), ()))
    down_part = lax.dot_general(scaled, hidden, first, preferred_element_type=jnp.float32)
    grad_hidden = lax.dot_general(scaled, weight_down, second, preferred_element_type=jnp.float32)
    d_gate = (grad_hidden * pre_up * sigmoid_gate * (1.0 + pre_gate * (1.0 - sigmoid_gate))).astype(jnp.bfloat16)
    d_up = (grad_hidden * silu_gate).astype(jnp.bfloat16)
    gate_part = lax.dot_general(x_rows, d_gate, first, preferred_element_type=jnp.float32)
    up_part = lax.dot_general(x_rows, d_up, first, preferred_element_type=jnp.float32)
    dx_rows = lax.dot_general(d_gate, weight_gate, second, preferred_element_type=jnp.float32)
    dx_rows = dx_rows + lax.dot_general(d_up, weight_up, second, preferred_element_type=jnp.float32)
    return (dx_rows.astype(jnp.bfloat16), slot_score, gate_part.astype(jnp.bfloat16),
            up_part.astype(jnp.bfloat16), down_part.astype(jnp.bfloat16))


def reference(acts, grad_out, expert_of, slot_of, source_row, combine, w_gate, w_up, w_down):
    def one_section(section_inputs):
        acts_s, grad_s, expert_s, slot_s, source_s, combine_s, gate_s, up_s, down_s = section_inputs

        def one_expert(expert_inputs):
            expert_id, slot_rows, weight_gate, weight_up, weight_down = expert_inputs
            filled = slot_rows >= 0
            safe_rows = jnp.where(filled, slot_rows, 0).astype(jnp.int32)
            x_rows = jnp.where(filled[:, None], acts_s[safe_rows], jnp.zeros((), jnp.bfloat16))
            g_rows = jnp.where(filled[:, None], grad_s[safe_rows], jnp.zeros((), jnp.bfloat16))
            chosen = expert_s[safe_rows] == expert_id
            picked = jnp.sum(jnp.where(chosen, combine_s[safe_rows].astype(jnp.float32), 0.0), axis=1)
            slot_weight = jnp.where(filled, picked, 0.0).astype(jnp.bfloat16)
            state = forward_rows(x_rows, weight_gate, weight_up, weight_down)
            return backward_rows(x_rows, g_rows, slot_weight, state, weight_gate, weight_up, weight_down)

        dx_all, score_all, gate_part, up_part, down_part = lax.map(
            one_expert, (jnp.arange(EXPERTS, dtype=jnp.int32), source_s, gate_s, up_s, down_s))
        flat_index = (expert_s * CAP + slot_s).astype(jnp.int32)
        dx_flat = dx_all.reshape(EXPERTS * CAP, D)
        grad_acts_s = jnp.sum(dx_flat[flat_index].astype(jnp.float32), axis=1).astype(jnp.bfloat16)
        grad_combine_s = score_all.reshape(EXPERTS * CAP)[flat_index]
        return grad_acts_s, grad_combine_s, gate_part, up_part, down_part

    grad_acts, grad_combine, gate_part, up_part, down_part = lax.map(
        one_section, (acts, grad_out, expert_of, slot_of, source_row, combine, w_gate, w_up, w_down))
    grad_gate = (gate_part.astype(jnp.float32) + gate_part[::-1].astype(jnp.float32)).astype(jnp.bfloat16)
    grad_up = (up_part.astype(jnp.float32) + up_part[::-1].astype(jnp.float32)).astype(jnp.bfloat16)
    down_sum = (down_part.astype(jnp.float32) + down_part[::-1].astype(jnp.float32)).astype(jnp.bfloat16)
    grad_down = jnp.swapaxes(down_sum, 2, 3)
    return grad_acts, grad_combine, grad_gate, grad_up, grad_down
```

```python
import jax
import jax.numpy as jnp
from jax import lax
from jax.experimental import pallas as pl
from jax.experimental.pallas import tpu as pltpu
from jax.sharding import PartitionSpec as P

BF = jnp.bfloat16
F32 = jnp.float32
RING = 8
LANES = 4


def ring_step(step):
    return [
        (z * LANES + lane, ((z + step) % RING) * LANES + lane)
        for z in range(RING)
        for lane in range(LANES)
    ]


COLUMN_GROUPS = [
    [z * LANES + 2 * col + core for z in range(RING) for core in range(2)] for col in range(2)
]
ACROSS = [(e, e ^ 2) for e in range(RING * LANES)]
FIRST = (((0,), (0,)), ((), ()))
SECOND = (((1,), (1,)), ((), ()))


def dot(a, b, dims=(((1,), (0,)), ((), ()))):
    return lax.dot_general(a, b, dims, preferred_element_type=F32)


ANYWHERE = pl.BlockSpec(memory_space=pl.ANY)
WHOLE = pl.BlockSpec(memory_space=pltpu.VMEM)
LIGHT = pl.CostEstimate(flops=1, bytes_accessed=1, transcendentals=0)
PARAMS = pltpu.CompilerParams(vmem_limit_bytes=40 * 1024 * 1024)
TILE = 512


def tie(value, after):
    def body(value_ref, *refs):
        refs[-1][...] = value_ref[...]

    return pl.pallas_call(
        body,
        out_shape=jax.ShapeDtypeStruct(value.shape, value.dtype),
        in_specs=[WHOLE] + [ANYWHERE] * len(after),
        out_specs=WHOLE,
        cost_estimate=LIGHT,
        compiler_params=PARAMS,
    )(value, *after)


def by_columns(body, rows, arrays, out_rows, after=()):
    width = arrays[0].shape[1]

    def inner(*refs):
        n, m = len(rows), len(arrays)
        body(refs[:n], refs[n : n + m], refs[n + m + len(after) :])

    def columns(count):
        return pl.BlockSpec((count, TILE), lambda i: (0, i))

    return pl.pallas_call(
        inner,
        grid=(width // TILE,),
        out_shape=[jax.ShapeDtypeStruct((n, width), BF) for n in out_rows],
        in_specs=[pl.BlockSpec(r.shape, lambda i: (0, 0)) for r in rows]
        + [columns(a.shape[0]) for a in arrays]
        + [ANYWHERE] * len(after),
        out_specs=[columns(n) for n in out_rows],
        cost_estimate=LIGHT,
        compiler_params=PARAMS,
    )(*rows, *arrays, *after)


def pick(rows_ref, tokens_ref):
    count = tokens_ref.shape[0]
    names = lax.broadcasted_iota(jnp.int32, (count, rows_ref.shape[1]), 0)
    hot = (names == rows_ref[...]).astype(F32).astype(BF)
    return dot(hot, tokens_ref[...], FIRST).astype(BF)


def pick_lanes(rows, tokens, most, after=()):
    def body(row_refs, token_refs, outs):
        for i, ref in enumerate(token_refs):
            picked = pick(row_refs[i % len(rows)], ref)
            for r in range(LANES):
                outs[r][i * most : (i + 1) * most, :] = picked[r * most : (r + 1) * most]

    return by_columns(body, rows, tokens, [len(tokens) * most] * LANES, after)


def pick_onward(rows_up, rows_down, tokens, most):
    full = LANES * most
    half = full // 2

    def body(row_refs, token_refs, outs):
        for d in range(2):
            for t in range(2):
                picked = pick(row_refs[d], token_refs[2 * d + t])
                outs[d][t * full : (t + 1) * full, :] = picked[:full]
                low = 2 * full + t * half
                outs[d][low : low + half, :] = picked[full:]

    return by_columns(body, [rows_up, rows_down], tokens, [3 * full] * 2)


def spread_far(up, down, most):
    full = LANES * most

    def body(_, refs, outs):
        for r in range(LANES):
            for t in range(2):
                for d in range(2):
                    at = (2 * t + d) * most
                    low = t * full + r * most
                    outs[r][at : at + most, :] = refs[d][low : low + most, :]

    return by_columns(body, [], [up, down], [4 * most] * LANES)


def spread_last(up, down, most):
    half = most // 2

    def body(_, refs, outs):
        for r in range(LANES):
            for t in range(2):
                for d in range(2):
                    at = (2 * t + d) * half
                    low = (t * LANES + r) * half
                    outs[r][at : at + half, :] = refs[d][low : low + half, :]

    return by_columns(body, [], [up, down], [2 * most] * LANES)


def chunk_grads(blocks, slot_weight, weight_gate, weight_up, weight_down, after=()):
    size = blocks[0].shape[0] // 2
    count = LANES * size
    width = blocks[0].shape[1]
    ff = weight_gate.shape[1]

    def body(*refs):
        w_ref, gate_ref, up_ref, down_ref = refs[LANES : LANES + 4]
        hidden_ref, d_ref, score_ref, x_ref, g_ref = refs[LANES + 4 + len(after) :]
        for r in range(LANES):
            x_ref[r * size : (r + 1) * size, :] = refs[r][:size, :]
            g_ref[r * size : (r + 1) * size, :] = refs[r][size:, :]
        pre_gate = dot(x_ref[...], gate_ref[...])
        pre_up = dot(x_ref[...], up_ref[...])
        sig = jax.nn.sigmoid(pre_gate)
        silu = pre_gate * sig
        hidden = (silu * pre_up).astype(BF)
        hidden_ref[...] = hidden
        g_wide = g_ref[...].astype(F32)
        expert_out = dot(hidden, down_ref[...])
        score_ref[...] = jnp.sum(expert_out * g_wide, axis=1, keepdims=True)
        scaled = (w_ref[...] * g_wide).astype(BF)
        grad_hidden = dot(scaled, down_ref[...], SECOND)
        d_ref[:, :ff] = (grad_hidden * pre_up * sig * (1.0 + pre_gate * (1.0 - sig))).astype(BF)
        d_ref[:, ff:] = (grad_hidden * silu).astype(BF)

    return pl.pallas_call(
        body,
        out_shape=[
            jax.ShapeDtypeStruct((count, ff), BF),
            jax.ShapeDtypeStruct((count, 2 * ff), BF),
            jax.ShapeDtypeStruct((count, 1), F32),
        ],
        in_specs=[WHOLE] * (LANES + 4) + [ANYWHERE] * len(after),
        out_specs=[WHOLE] * 3,
        scratch_shapes=[pltpu.VMEM((count, width), BF), pltpu.VMEM((count, width), BF)],
        cost_estimate=LIGHT,
        compiler_params=PARAMS,
    )(*blocks, slot_weight, weight_gate, weight_up, weight_down, *after)


def weight_grads(chunks, slot_weight, hidden, d_both):
    blocks = [b for chunk in chunks for b in chunk]
    sizes = [b.shape[0] // 2 for b in blocks]
    count, ff = hidden.shape
    width = blocks[0].shape[1]
    tile = 256

    def body(*refs):
        w_ref, hidden_ref, d_ref = refs[len(blocks) : len(blocks) + 3]
        gate_ref, up_ref, down_ref, x_ref, g_ref = refs[len(blocks) + 3 :]
        at = 0
        for ref, size in zip(refs, sizes):
            x_ref[at : at + size, :] = ref[:size, :]
            g_ref[at : at + size, :] = ref[size:, :]
            at += size
        scaled = (w_ref[...] * g_ref[...].astype(F32)).astype(BF)
        down_ref[...] = dot(hidden_ref[...], scaled, FIRST).astype(BF)
        both = dot(x_ref[...], d_ref[...], FIRST).astype(BF)
        gate_ref[...] = both[:, :ff]
        up_ref[...] = both[:, ff:]

    def fixed(a):
        return pl.BlockSpec(a.shape, lambda i: (0, 0))

    return pl.pallas_call(
        body,
        grid=(width // tile,),
        out_shape=[
            jax.ShapeDtypeStruct((width, ff), BF),
            jax.ShapeDtypeStruct((width, ff), BF),
            jax.ShapeDtypeStruct((ff, width), BF),
        ],
        in_specs=[pl.BlockSpec((b.shape[0], tile), lambda i: (0, i)) for b in blocks]
        + [fixed(slot_weight), fixed(hidden), fixed(d_both)],
        out_specs=[
            pl.BlockSpec((tile, ff), lambda i: (i, 0)),
            pl.BlockSpec((tile, ff), lambda i: (i, 0)),
            pl.BlockSpec((ff, tile), lambda i: (0, i)),
        ],
        scratch_shapes=[pltpu.VMEM((count, tile), BF), pltpu.VMEM((count, tile), BF)],
        cost_estimate=LIGHT,
        compiler_params=PARAMS,
    )(*blocks, slot_weight, hidden, d_both)


def turn(blocks, z):
    return lax.dynamic_slice_in_dim(jnp.concatenate([blocks, blocks]), z, RING, 0)


def lanes_from_own(blocks, lane):
    swapped = jnp.stack([blocks[:, r ^ 1] for r in range(LANES)], axis=1)
    blocks = jnp.where(lane % 2 == 1, swapped, blocks)
    swapped = jnp.stack([blocks[:, r ^ 2] for r in range(LANES)], axis=1)
    return jnp.where(lane // 2 == 1, swapped, blocks)


def per_device(acts, grad_out, expert_of, slot_of, source_row, combine, w_gate, w_up, w_down):
    me = lax.axis_index("expert")
    z = me // LANES
    lane = me % LANES
    col = lane // 2
    tok = acts.shape[1]
    width = acts.shape[2]
    experts = source_row.shape[1]
    most = source_row.shape[2]
    sections = lax.axis_size("section")
    weight_gate = w_gate[0, 0]
    weight_up = w_up[0, 0]
    weight_down = w_down[0, 0]
    up_ring = ring_step(1)
    down_ring = ring_step(-1)

    own = (acts[0], grad_out[0])
    plus1 = [lax.ppermute(t, "expert", up_ring) for t in own]
    minus1 = [lax.ppermute(t, "expert", down_ring) for t in own]

    place = expert_of[0] * most + (slot_of[0] - me * most)
    place_across = lax.ppermute(place, "expert", ACROSS)
    hit = place.reshape(-1, 1) == jnp.arange(experts * most, dtype=jnp.int32)[None, :]
    slot_weight = jnp.sum(jnp.where(hit, combine[0].reshape(-1, 1).astype(F32), 0.0), axis=0)
    local = jnp.where(source_row[0] >= 0, source_row[0] - me * tok, -1).astype(BF)
    planes = lanes_from_own(turn(local.reshape(RING, LANES, most), z), lane)
    message = jnp.concatenate(
        [
            slot_weight.astype(BF).reshape(experts, most),
            jnp.broadcast_to(planes.reshape(1, -1), (experts, experts * most)),
        ],
        axis=1,
    )
    arrived = lax.all_to_all(tie(message, [plus1[0], minus1[0]]), "expert", 0, 0, tiled=True)
    arrived = turn(arrived.reshape(RING, LANES, most + experts * most), z)
    weights = lanes_from_own(arrived[:, :, :most], lane)
    table = lax.dynamic_slice_in_dim(arrived[:, :, most:], lane, 1, 1)
    table = table.astype(jnp.int32).reshape(RING, RING, LANES, most)

    def rows_of(offset, plane):
        return table[offset % RING, (plane - offset) % RING]

    def flat(*pieces):
        return jnp.concatenate([p.reshape(1, -1) for p in pieces], axis=1)

    def exchange(blocks):
        return [blocks[0]] + [
            lax.ppermute(blocks[r], "expert", [(e, e ^ r) for e in range(experts)])
            for r in (1, 2, 3)
        ]

    def weights_at(offsets):
        w_rows = jnp.stack([weights[o % RING] for o in offsets], axis=1)
        return w_rows.reshape(-1, 1).astype(F32)

    expert_weights = (weight_gate, weight_up, weight_down)
    offsets_of = ((0, -1, 1), (-2, 2), (-3, 3), (4,))
    w_chunk = [weights_at(offsets) for offsets in offsets_of]
    half = most // 2
    plus2 = [lax.ppermute(t, "expert", up_ring) for t in plus1]
    minus2 = [lax.ppermute(t, "expert", down_ring) for t in minus1]
    near_out = pick_lanes(
        [flat(rows_of(o, 0)) for o in offsets_of[0]],
        [own[0], plus1[0], minus1[0], own[1], plus1[1], minus1[1]],
        most,
    )
    near = exchange(near_out)

    onward_up, onward_down = pick_onward(
        flat(rows_of(-2, 1), rows_of(-2, 2)[:, :half]),
        flat(rows_of(2, -1), rows_of(2, -2)[:, half:]),
        [plus2[0], plus2[1], minus2[0], minus2[1]],
        most,
    )
    plus3 = lax.ppermute(onward_up, "expert", up_ring)
    minus3 = lax.ppermute(onward_down, "expert", down_ring)
    mid_out = pick_lanes(
        [flat(rows_of(o, 0)) for o in offsets_of[1]],
        [plus2[0], minus2[0], plus2[1], minus2[1]],
        most,
        after=[onward_up],
    )
    mid = exchange(mid_out)
    near_done = chunk_grads(near, w_chunk[0], *expert_weights, after=[mid_out[3]])

    low = 2 * LANES * most
    plus4 = lax.ppermute(plus3[low:], "expert", up_ring)
    minus4 = lax.ppermute(minus3[low:], "expert", down_ring)
    far_out = spread_far(plus3, minus3, most)
    far = exchange(far_out)
    mid_done = chunk_grads(mid, w_chunk[1], *expert_weights, after=[far_out[3]])

    last_out = spread_last(plus4, minus4, most)
    last = exchange(last_out)
    far_done = chunk_grads(far, w_chunk[2], *expert_weights, after=[last_out[3]])
    last_done = chunk_grads(last, w_chunk[3], *expert_weights)

    hidden, d_rows, score = [
        jnp.concatenate(pieces) for pieces in zip(near_done, mid_done, far_done, last_done)
    ]
    gate_part, up_part, down_part = weight_grads(
        [near, mid, far, last], jnp.concatenate(w_chunk), hidden, d_rows
    )
    mirror = [(s, sections - 1 - s) for s in range(sections)]
    gate_far, up_far, down_far = [
        lax.ppermute(part, "section", mirror) for part in (gate_part, up_part, down_part)
    ]

    def row_at(source_z, source_lane, slot):
        offset = (source_z - z + RING) % RING
        apart = source_lane ^ lane
        row = jnp.zeros_like(offset + apart + slot)
        base = 0
        for offsets in offsets_of:
            count = len(offsets)
            for i, o in enumerate(offsets):
                here = base * LANES * most + (apart * count + i) * most + slot
                row = jnp.where(offset == o % RING, here, row)
            base += count
        return row

    slots = jnp.arange(experts * most, dtype=jnp.int32)
    ring_at = slots // (4 * most)
    core_at = (slots // (2 * most)) % 2
    col_at = (slots // most) % 2

    def collect(place_of, from_col):
        wanted = (ring_at * LANES + col * 2 + core_at) * most + slots % most
        mine = col_at == from_col
        hot = jnp.zeros((tok, experts * most), jnp.bool_)
        for k in range(2):
            hot = hot | (place_of[:, k : k + 1] == wanted[None, :])
        return (hot & mine[None, :]).astype(BF)

    d_rows = tie(d_rows, [gate_part])
    order = row_at(ring_at, col_at * 2 + core_at, slots % most)
    hot_order = (order[:, None] == slots[None, :]).astype(BF)
    d_both = dot(hot_order, d_rows).astype(BF)
    ff = weight_gate.shape[1]
    hot_own = collect(place, col)
    hot_across = collect(place_across, 1 - col)
    pieces = []
    cut = width // 2
    for i in range(2):
        span = slice(i * cut, (i + 1) * cut)
        dx = dot(d_both[:, :ff], weight_gate[span], SECOND)
        dx = (dx + dot(d_both[:, ff:], weight_up[span], SECOND)).astype(BF)
        back = lax.all_to_all(
            dx.reshape(2 * RING, 2 * most, cut),
            "expert",
            0,
            0,
            tiled=True,
            axis_index_groups=COLUMN_GROUPS,
        ).reshape(-1, cut)
        away = lax.ppermute(dot(hot_across, back).astype(BF), "expert", ACROSS)
        here = dot(hot_own, back)
        pieces.append((here + away.astype(F32)).astype(BF))
    grad_acts = jnp.concatenate(pieces, axis=1)
    by_expert = row_at(slots // (LANES * most), (slots // most) % LANES, slots % most)
    match = by_expert[:, None] == slots[None, :]
    scores = jnp.sum(jnp.where(match, score.reshape(1, -1), 0.0), axis=1).astype(BF)
    scores = tie(scores.reshape(experts, most), [back])
    score_back = lax.all_to_all(scores, "expert", 0, 0, tiled=True).reshape(-1)
    found = jnp.where(hit, score_back[None, :].astype(F32), 0.0)
    grad_combine = jnp.sum(found, axis=1).astype(BF).reshape(tok, 2)

    def total(a, b):
        return (a.astype(F32) + b.astype(F32)).astype(BF)[None, None]

    return (
        grad_acts[None],
        grad_combine[None],
        total(gate_part, gate_far),
        total(up_part, up_far),
        total(down_part, down_far),
    )


def solution(mesh):
    return jax.shard_map(
        per_device,
        mesh=mesh,
        in_specs=(
            P("section", "expert", None),
            P("section", "expert", None),
            P("section", "expert", None),
            P("section", "expert", None),
            P("section", None, "expert"),
            P("section", "expert", None),
            P("section", "expert", None, None),
            P("section", "expert", None, None),
            P("section", "expert", None, None),
        ),
        out_specs=(
            P("section", "expert", None),
            P("section", "expert", None),
            P("section", "expert", None, None),
            P("section", "expert", None, None),
            P("section", "expert", None, None),
        ),
        check_vma=False,
    )
```

```python
import jax
import jax.numpy as jnp
from jax import lax
from jax.experimental import pallas as pl
from jax.experimental.pallas import tpu as pltpu
from jax.sharding import PartitionSpec as P

BF = jnp.bfloat16
F32 = jnp.float32
RING = 8
LANES = 4


def ring_step(step):
    return [
        (z * LANES + lane, ((z + step) % RING) * LANES + lane)
        for z in range(RING)
        for lane in range(LANES)
    ]


PLANE_GROUPS = [[z * LANES + lane for lane in range(LANES)] for z in range(RING)]
COLUMN_GROUPS = [
    [z * LANES + 2 * col + core for z in range(RING) for core in range(2)] for col in range(2)
]
ACROSS = [(e, e ^ 2) for e in range(RING * LANES)]
FIRST = (((0,), (0,)), ((), ()))
SECOND = (((1,), (1,)), ((), ()))


def dot(a, b, dims=(((1,), (0,)), ((), ()))):
    return lax.dot_general(a, b, dims, preferred_element_type=F32)


ROUTE_ROWS = 16
SCORE = 128
ANYWHERE = pl.BlockSpec(memory_space=pl.ANY)
WHOLE = pl.BlockSpec(memory_space=pltpu.VMEM)
LIGHT = pl.CostEstimate(flops=1, bytes_accessed=1, transcendentals=0)
PARAMS = pltpu.CompilerParams(vmem_limit_bytes=63 * 1024 * 1024)
TILE = 512


def route_rows(acts, source_row, expert_of, combine, me):
    tok, width = acts.shape
    most = source_row.shape[1]
    slots = LANES * most

    def body(me_ref, acts_ref, source_ref, expert_ref, combine_ref, out_ref, table_ref):
        own = me_ref[0]
        own_z = own // LANES
        out_ref[:tok, :] = acts_ref[...]
        names = lax.broadcasted_iota(jnp.int32, (tok, slots), 0)
        which = lax.broadcasted_iota(jnp.int32, (1, slots), 1) // most
        wide = combine_ref[...].astype(F32)
        for p in range(RING):
            plane = lax.rem(own_z + p, RING) * LANES
            for r in range(LANES):
                row = source_ref[pl.ds(plane + r, 1), :]
                row = jnp.where(row >= 0, row - own * tok, -1)
                table_ref[p : p + 1, r * most : (r + 1) * most] = row.astype(F32)
            hot = names == table_ref[p : p + 1, :].astype(jnp.int32)
            expert = plane + which
            weight = jnp.zeros((tok, slots), F32)
            for k in range(2):
                chosen = expert_ref[:, k : k + 1] == expert
                weight = weight + jnp.where(chosen, wide[:, k : k + 1], 0.0)
            weight = jnp.sum(jnp.where(hot, weight, 0.0), axis=0, keepdims=True)
            table_ref[RING + p : RING + p + 1, :] = weight
        out_ref[tok:, :] = jnp.zeros((ROUTE_ROWS, width), BF)
        out_ref[tok:, :slots] = table_ref[...].astype(BF)

    return pl.pallas_call(
        body,
        out_shape=jax.ShapeDtypeStruct((tok + ROUTE_ROWS, width), BF),
        in_specs=[pl.BlockSpec(memory_space=pltpu.SMEM)] + [WHOLE] * 4,
        out_specs=WHOLE,
        scratch_shapes=[pltpu.VMEM((ROUTE_ROWS, slots), F32)],
        cost_estimate=LIGHT,
        compiler_params=PARAMS,
    )(me.reshape(1), acts, source_row, expert_of, combine)


def pick(route, plane, x_ref, g_ref):
    tok = g_ref.shape[0]
    names = route[plane : plane + 1, :].astype(jnp.int32)
    index = lax.broadcasted_iota(jnp.int32, (tok, names.shape[1]), 0)
    hot = index == names
    weight = jnp.where(hot, route[RING + plane : RING + plane + 1, :], 0.0).astype(BF)
    x = dot(hot.astype(F32).astype(BF), x_ref[:tok, :], FIRST).astype(BF)
    return x, dot(weight, g_ref[...], FIRST).astype(BF)


def pick_call(body, sources, out_rows, after):
    tok, width = sources[0][1].shape
    count = len(sources)
    slots = LANES * 32

    def inner(*refs):
        routes = [r[:, :slots].astype(F32) for r in refs[:count]]
        outs = refs[3 * count + len(after) :]
        body(routes, refs[count : 2 * count], refs[2 * count : 3 * count], outs)

    def columns(rows):
        return pl.BlockSpec((rows, TILE), lambda i: (0, i))

    xs = [x for x, _ in sources]
    gs = [g for _, g in sources]
    return pl.pallas_call(
        inner,
        grid=(width // TILE,),
        out_shape=[jax.ShapeDtypeStruct((n, width), BF) for n in out_rows],
        in_specs=[pl.BlockSpec((ROUTE_ROWS, TILE), lambda i: (tok // ROUTE_ROWS, 0))] * count
        + [columns(tok + ROUTE_ROWS)] * count
        + [columns(tok)] * count
        + [ANYWHERE] * len(after),
        out_specs=[columns(n) for n in out_rows],
        cost_estimate=LIGHT,
        compiler_params=PARAMS,
    )(*xs, *xs, *gs, *after)


def pick_lanes(sources, planes, most, after=()):
    size = len(sources) * 2 * most

    def body(routes, x_refs, g_refs, outs):
        for i in range(len(sources)):
            for t, rows in enumerate(pick(routes[i], planes[i], x_refs[i], g_refs[i])):
                for r in range(LANES):
                    at = r * size + (2 * i + t) * most
                    outs[0][at : at + most, :] = rows[r * most : (r + 1) * most]

    return pick_call(body, sources, [LANES * size], after)[0]


def pick_onward(sources, planes, most, after=()):
    half = most // 2
    low = 2 * LANES * most

    def body(routes, x_refs, g_refs, outs):
        for d in range(2):
            for t, rows in enumerate(pick(routes[d], planes[d][0], x_refs[d], g_refs[d])):
                for r in range(LANES):
                    to = (2 * r + t) * most
                    outs[d][to : to + most, :] = rows[r * most : (r + 1) * most]
            for t, rows in enumerate(pick(routes[d], planes[d][1], x_refs[d], g_refs[d])):
                for r in range(LANES):
                    to, at = low + (2 * r + t) * half, r * most + d * half
                    outs[d][to : to + half, :] = rows[at : at + half]

    return pick_call(body, sources, [low + low // 2] * 2, after)


def spread(up, down, rows, onward, after=()):
    width = up.shape[1]
    rest = up.shape[0] - rows
    size = rows // LANES

    def body(up_ref, down_ref, *refs):
        outs = refs[len(after) :]
        for r in range(LANES):
            for i, ref in enumerate((up_ref, down_ref)):
                to = (2 * r + i) * size
                outs[0][to : to + size, :] = ref[r * size : (r + 1) * size, :]
        if onward:
            outs[1][...] = up_ref[rows:, :]
            outs[2][...] = down_ref[rows:, :]

    shapes = [2 * rows] + [rest] * (2 * onward)

    def columns(count):
        return pl.BlockSpec((count, TILE), lambda i: (0, i))

    return pl.pallas_call(
        body,
        grid=(width // TILE,),
        out_shape=[jax.ShapeDtypeStruct((n, width), BF) for n in shapes],
        in_specs=[columns(up.shape[0])] * 2 + [ANYWHERE] * len(after),
        out_specs=[columns(n) for n in shapes],
        cost_estimate=LIGHT,
        compiler_params=PARAMS,
    )(up, down, *after)


def collect(back, place, lane_info, width):
    slots = back.shape[0]
    tok = place.shape[0]

    def body(info_ref, place_ref, back_ref, out_ref):
        slot = lax.broadcasted_iota(jnp.int32, (tok, slots), 1)
        most = 32
        expert = (slot // (4 * most)) * LANES + info_ref[0] * 2 + (slot // (2 * most)) % 2
        wanted = expert * most + slot % most
        wanted = jnp.where((slot // most) % 2 == info_ref[1], wanted, -1)
        hots = [place_ref[:, k : k + 1] == wanted for k in range(2)]
        hots = [h.astype(F32) for h in hots]
        both = (hots[0] + hots[1]).astype(BF)
        out_ref[:, :width] = dot(both, back_ref[:, :width]).astype(out_ref.dtype)
        tail = back_ref[:, width:]
        scores = [dot(h.astype(BF), tail) for h in hots]
        at = lax.broadcasted_iota(jnp.int32, scores[0].shape, 1)
        kept = jnp.where(at < 2, scores[0], jnp.where(at < 4, scores[1], 0.0))
        out_ref[:, width:] = kept.astype(out_ref.dtype)

    return pl.pallas_call(
        body,
        out_shape=jax.ShapeDtypeStruct((tok, back.shape[1]), BF),
        in_specs=[pl.BlockSpec(memory_space=pltpu.SMEM), WHOLE, WHOLE],
        out_specs=WHOLE,
        cost_estimate=LIGHT,
        compiler_params=PARAMS,
    )(jnp.stack(lane_info), place, back)


def chunk_grads(block, run, start, total_rows, places, shared, weights, after=()):
    rows, width = block.shape
    rows = rows // LANES
    size = rows // 2
    count = LANES * size
    ff = weights[0].shape[1]
    most = 32
    runs = size // run
    n_in = 2 + 3 + len(after) + len(shared)

    def body(*refs):
        place_ref = refs[0]
        gate_ref, up_ref, down_ref = refs[2:5]
        outs = refs[n_in : n_in + 5]
        x, g, hid, d, dx, wg, wu, wd, sems, out_sems = refs[n_in + 5 :]
        loads = [
            pltpu.make_async_copy(gate_ref, wg, sems.at[0]),
            pltpu.make_async_copy(up_ref, wu, sems.at[1]),
            pltpu.make_async_copy(down_ref, wd, sems.at[2]),
        ]
        pieces = []
        for t, into in enumerate((x, g)):
            for r in range(LANES):
                for i in range(runs):
                    pieces.append(
                        pltpu.make_async_copy(
                            refs[1].at[pl.ds(r * rows + (2 * i + t) * run, run), :],
                            into.at[pl.ds(r * size + i * run, run), :],
                            sems.at[3 + len(pieces)],
                        )
                    )
        split = len(pieces) // 2
        for copy in pieces[:split] + loads[:2] + pieces[split:] + loads[2:]:
            copy.start()
        stores = []

        def store(part, ref):
            stores.append(pltpu.make_async_copy(part, ref, out_sems.at[len(stores)]))
            stores[-1].start()

        mine = pl.ds(start, count)
        for copy in pieces[:split]:
            copy.wait()
        store(x, outs[0].at[mine, :])
        loads[0].wait()
        pre_gate = dot(x[...], wg[...])
        loads[1].wait()
        pre_up = dot(x[...], wu[...])
        sig = jax.nn.sigmoid(pre_gate)
        silu = pre_gate * sig
        hidden = silu * pre_up
        hid[...] = hidden.astype(BF)
        store(hid, outs[2].at[mine, :])
        for copy in pieces[split:]:
            copy.wait()
        store(g, outs[1].at[mine, :])
        loads[2].wait()
        grad_hidden = dot(g[...], wd[...], SECOND)
        score = jnp.sum(hid[...].astype(F32) * grad_hidden, axis=1, keepdims=True)
        high = score.astype(BF).astype(F32)
        at = lax.broadcasted_iota(jnp.int32, (count, SCORE), 1)
        tail = jnp.where(at % 2 == 0, high, score - high)
        dx[:, width:] = jnp.where(at < 4, tail, 0.0).astype(BF)
        d_gate = (grad_hidden * pre_up * sig * (1.0 + pre_gate * (1.0 - sig))).astype(BF)
        d_up = (grad_hidden * silu).astype(BF)
        d[:, :ff] = d_gate
        d[:, ff:] = d_up
        store(d, outs[3].at[mine, :])
        back = dot(d_gate, wg[...], SECOND) + dot(d_up, wu[...], SECOND)
        dx[:, :width] = back.astype(BF)
        for b in range(count // most):
            to = pl.multiple_of(place_ref[b], most)
            store(dx.at[pl.ds(b * most, most), :], outs[4].at[pl.ds(to, most), :])
        for copy in stores:
            copy.wait()

    shapes = [width, width, ff, 2 * ff, width + SCORE]
    first = 5 + len(after)
    return pl.pallas_call(
        body,
        out_shape=[jax.ShapeDtypeStruct((total_rows, n), BF) for n in shapes],
        in_specs=[pl.BlockSpec(memory_space=pltpu.SMEM)] + [ANYWHERE] * (n_in - 1),
        out_specs=[ANYWHERE] * 5,
        input_output_aliases={first + i: i for i in range(len(shared))},
        scratch_shapes=[
            pltpu.VMEM((count, width), BF),
            pltpu.VMEM((count, width), BF),
            pltpu.VMEM((count, ff), BF),
            pltpu.VMEM((count, 2 * ff), BF),
            pltpu.VMEM((count, width + SCORE), BF),
            pltpu.VMEM((width, ff), BF),
            pltpu.VMEM((width, ff), BF),
            pltpu.VMEM((ff, width), BF),
            pltpu.SemaphoreType.DMA((3 + 2 * LANES * runs,)),
            pltpu.SemaphoreType.DMA((4 + count // most,)),
        ],
        cost_estimate=LIGHT,
        compiler_params=PARAMS,
    )(places, block, *weights, *after, *shared)


def weight_grads(left, right, across, after=()):
    count = left.shape[0]
    shape = (left.shape[1], right.shape[1])
    tile = 512

    def body(left_ref, right_ref, *refs):
        refs[-1][...] = dot(left_ref[...], right_ref[...], FIRST).astype(BF)

    def fixed(a):
        return pl.BlockSpec(a.shape, lambda i: (0, 0))

    moving = pl.BlockSpec((count, tile), lambda i: (0, i))

    return pl.pallas_call(
        body,
        grid=(shape[1] // tile if across else shape[0] // tile,),
        out_shape=jax.ShapeDtypeStruct(shape, BF),
        in_specs=([fixed(left), moving] if across else [moving, fixed(right)])
        + [ANYWHERE] * len(after),
        out_specs=pl.BlockSpec((shape[0], tile), lambda i: (0, i))
        if across
        else pl.BlockSpec((tile, shape[1]), lambda i: (i, 0)),
        cost_estimate=LIGHT,
        compiler_params=PARAMS,
    )(left, right, *after)


def total(a, b, parts, after):
    rows, columns = a.shape
    tile, part = rows // 4, columns // parts

    def body(a_ref, b_ref, *refs):
        both = (a_ref[...].astype(F32) + b_ref[...].astype(F32)).astype(BF)
        for i in range(parts):
            refs[len(after) + i][...] = both[:, i * part : (i + 1) * part]

    def block(count):
        return pl.BlockSpec((tile, count), lambda i: (i, 0))

    return pl.pallas_call(
        body,
        grid=(4,),
        out_shape=[jax.ShapeDtypeStruct((rows, part), BF)] * parts,
        in_specs=[block(columns)] * 2 + [ANYWHERE] * len(after),
        out_specs=[block(part)] * parts,
        cost_estimate=LIGHT,
        compiler_params=PARAMS,
    )(a, b, *after)


def per_device(acts, grad_out, expert_of, slot_of, source_row, combine, w_gate, w_up, w_down):
    me = lax.axis_index("expert")
    z = me // LANES
    col = (me // 2) % 2
    tok = acts.shape[1]
    width = acts.shape[2]
    experts = source_row.shape[1]
    most = source_row.shape[2]
    sections = lax.axis_size("section")
    weight_gate = w_gate[0, 0]
    weight_up = w_up[0, 0]
    weight_down = w_down[0, 0]
    up_ring = ring_step(1)
    down_ring = ring_step(-1)

    place = expert_of[0] * most + (slot_of[0] - me * most)
    place_across = lax.ppermute(place, "expert", ACROSS)
    routed = route_rows(acts[0], source_row[0], expert_of[0], combine[0], me)
    own = (routed, grad_out[0])
    plus1 = [lax.ppermute(t, "expert", up_ring) for t in own]
    minus1 = [lax.ppermute(t, "expert", down_ring) for t in own]
    plus2 = [lax.ppermute(t, "expert", up_ring) for t in plus1]
    minus2 = [lax.ppermute(t, "expert", down_ring) for t in minus1]

    def exchange(block):
        return lax.all_to_all(
            block, "expert", 0, 0, tiled=True, axis_index_groups=PLANE_GROUPS
        )

    slot_count = experts * most
    offsets_of = ((0,), (-1, 1), (-2, 2), (-3, 3), (4,))
    starts = [b * LANES * most for b in (0, 1, 3, 5, 7)]

    def places(offsets):
        found = []
        for other in range(LANES):
            for o in offsets:
                ring = (z + o + RING) % RING
                found.append(((ring * 2 + other % 2) * 2 + other // 2) * most)
        return jnp.stack(found).astype(jnp.int32)

    expert_weights = (weight_gate, weight_up, weight_down)

    def work(i, blocks, run, shared, after=()):
        return chunk_grads(
            blocks, run, starts[i], slot_count, places(offsets_of[i]), shared, expert_weights, after
        )

    own_out = pick_lanes([own], [0], most, after=[place_across])
    here_rows = exchange(own_out)
    shared = work(0, here_rows, most, [])
    near_out = pick_lanes(
        [plus1, minus1], [1, RING - 1], most, after=[shared[4], plus2[0], minus2[0]]
    )
    near = exchange(near_out)
    onward_up, onward_down = pick_onward(
        [plus2, minus2], [[3, 4], [RING - 3, RING - 4]], most, after=[near_out]
    )
    plus3 = lax.ppermute(onward_up, "expert", up_ring)
    minus3 = lax.ppermute(onward_down, "expert", down_ring)
    mid_out = pick_lanes([plus2, minus2], [2, RING - 2], most, after=[onward_up])
    mid = exchange(mid_out)
    shared = work(1, near, most, shared, after=[mid_out])
    far_out, last_up, last_down = spread(
        plus3, minus3, 2 * LANES * most, True, after=[shared[4]]
    )
    plus4 = lax.ppermute(last_up, "expert", up_ring)
    minus4 = lax.ppermute(last_down, "expert", down_ring)
    far = exchange(far_out)
    shared = work(2, mid, most, shared, after=[far_out])
    (last_out,) = spread(plus4, minus4, LANES * most, False, after=[shared[4]])
    last = exchange(last_out)
    shared = work(3, far, most, shared, after=[last_out])
    shared = work(4, last, most // 2, shared)

    x_all, g_all, hidden, d_rows, dx = shared
    down_part = weight_grads(hidden, g_all, True)
    in_parts = weight_grads(x_all, d_rows, False, after=[down_part])
    mirror = [(s, sections - 1 - s) for s in range(sections)]
    down_far = lax.ppermute(down_part, "section", mirror)
    in_far = lax.ppermute(in_parts, "section", mirror)

    back = lax.all_to_all(
        dx.reshape(2 * RING, 2 * most, width + SCORE),
        "expert",
        0,
        0,
        tiled=True,
        axis_index_groups=COLUMN_GROUPS,
    ).reshape(-1, width + SCORE)
    leaving = collect(back, place_across, [col, 1 - col], width)
    away = lax.ppermute(leaving, "expert", ACROSS)
    here = collect(back, place, [col, col], width)
    both = here.astype(F32) + away.astype(F32)
    grad_acts = both[:, :width].astype(BF)
    found = jnp.stack([both[:, width + 2 * k] + both[:, width + 2 * k + 1] for k in range(2)], 1)
    grad_combine = (found / combine[0].astype(F32)).astype(BF)
    (grad_down,) = total(down_part, down_far, 1, [leaving])
    grad_gate, grad_up = total(in_parts, in_far, 2, [grad_down])
    return (
        grad_acts[None],
        grad_combine[None],
        grad_gate[None, None],
        grad_up[None, None],
        grad_down[None, None],
    )


def solution(mesh):
    return jax.shard_map(
        per_device,
        mesh=mesh,
        in_specs=(
            P("section", "expert", None),
            P("section", "expert", None),
            P("section", "expert", None),
            P("section", "expert", None),
            P("section", None, "expert"),
            P("section", "expert", None),
            P("section", "expert", None, None),
            P("section", "expert", None, None),
            P("section", "expert", None, None),
        ),
        out_specs=(
            P("section", "expert", None),
            P("section", "expert", None),
            P("section", "expert", None, None),
            P("section", "expert", None, None),
            P("section", "expert", None, None),
        ),
        check_vma=False,
    )
```

```python
import jax
import jax.numpy as jnp
from jax import lax
from jax.experimental import pallas as pl
from jax.experimental.pallas import tpu as pltpu
from jax.sharding import PartitionSpec as P

BF = jnp.bfloat16
F32 = jnp.float32
RING = 8
LANES = 4


def ring_step(step):
    return [
        (z * LANES + lane, ((z + step) % RING) * LANES + lane)
        for z in range(RING)
        for lane in range(LANES)
    ]


PLANE_GROUPS = [[z * LANES + lane for lane in range(LANES)] for z in range(RING)]
COLUMN_GROUPS = [
    [z * LANES + 2 * col + core for z in range(RING) for core in range(2)] for col in range(2)
]
ACROSS = [(e, e ^ 2) for e in range(RING * LANES)]
FIRST = (((0,), (0,)), ((), ()))
SECOND = (((1,), (1,)), ((), ()))


def dot(a, b, dims=(((1,), (0,)), ((), ()))):
    return lax.dot_general(a, b, dims, preferred_element_type=F32)


ROUTE_ROWS = 16
SCORE = 128
ANYWHERE = pl.BlockSpec(memory_space=pl.ANY)
WHOLE = pl.BlockSpec(memory_space=pltpu.VMEM)
LIGHT = pl.CostEstimate(flops=1, bytes_accessed=1, transcendentals=0)
PARAMS = pltpu.CompilerParams(vmem_limit_bytes=63 * 1024 * 1024)
TILE = 512


def route_rows(acts, grads, source_row, experts_of, combine, me):
    tok, width = acts.shape
    most = source_row.shape[1]
    slots = LANES * most
    behind = tok + ROUTE_ROWS

    def body(me_ref, acts_ref, grads_ref, source_ref, expert_ref, combine_ref, out_ref, table):
        own = me_ref[0]
        own_z = own // LANES
        out_ref[:tok, :] = acts_ref[...]
        out_ref[behind:, :] = grads_ref[...]
        index = lax.broadcasted_iota(jnp.int32, (tok, slots), 0)
        which = lax.broadcasted_iota(jnp.int32, (1, slots), 1) // most
        experts = expert_ref[...].astype(F32).astype(BF)
        for p in range(RING):
            plane = lax.rem(own_z + p, RING) * LANES
            for r in range(LANES):
                row = source_ref[pl.ds(plane + r, 1), :]
                row = jnp.where(row >= 0, row - own * tok, -1)
                table[p : p + 1, r * most : (r + 1) * most] = row.astype(F32)
            hot = index == table[p : p + 1, :].astype(jnp.int32)
            hot = hot.astype(F32).astype(BF)
            named = dot(experts, hot)
            value = dot(combine_ref[...], hot)
            expert = (plane + which).astype(F32)
            weight = jnp.where(named == expert, value, 0.0)
            table[RING + p : RING + p + 1, :] = weight[0:1] + weight[1:2]
        out_ref[tok:behind, :] = jnp.zeros((ROUTE_ROWS, width), BF)
        out_ref[tok:behind, :slots] = table[...].astype(BF)

    return pl.pallas_call(
        body,
        out_shape=jax.ShapeDtypeStruct((behind + tok, width), BF),
        in_specs=[pl.BlockSpec(memory_space=pltpu.SMEM)] + [WHOLE] * 5,
        out_specs=WHOLE,
        scratch_shapes=[pltpu.VMEM((ROUTE_ROWS, slots), F32)],
        cost_estimate=LIGHT,
        compiler_params=PARAMS,
    )(me.reshape(1), acts, grads, source_row, experts_of, combine)


def pick(route, plane, ref):
    tok = (ref.shape[0] - ROUTE_ROWS) // 2
    names = route[plane : plane + 1, :].astype(jnp.int32)
    index = lax.broadcasted_iota(jnp.int32, (tok, names.shape[1]), 0)
    hot = index == names
    weight = jnp.where(hot, route[RING + plane : RING + plane + 1, :], 0.0).astype(BF)
    x = dot(hot.astype(F32).astype(BF), ref[:tok, :], FIRST).astype(BF)
    return x, dot(weight, ref[tok + ROUTE_ROWS :, :], FIRST).astype(BF)


def pick_call(body, sources, out_rows, after):
    rows, width = sources[0].shape
    tok = (rows - ROUTE_ROWS) // 2
    count = len(sources)
    slots = LANES * 32

    def inner(*refs):
        routes = [r[:, :slots].astype(F32) for r in refs[:count]]
        body(routes, refs[count : 2 * count], refs[2 * count + len(after) :])

    def columns(size):
        return pl.BlockSpec((size, TILE), lambda i: (0, i))

    return pl.pallas_call(
        inner,
        grid=(width // TILE,),
        out_shape=[jax.ShapeDtypeStruct((n, width), BF) for n in out_rows],
        in_specs=[pl.BlockSpec((ROUTE_ROWS, TILE), lambda i: (tok // ROUTE_ROWS, 0))] * count
        + [columns(rows)] * count
        + [ANYWHERE] * len(after),
        out_specs=[columns(n) for n in out_rows],
        cost_estimate=LIGHT,
        compiler_params=PARAMS,
    )(*sources, *sources, *after)


def pick_lanes(sources, planes, most, after=()):
    size = len(sources) * 2 * most

    def body(routes, refs, outs):
        for i in range(len(sources)):
            for t, rows in enumerate(pick(routes[i], planes[i], refs[i])):
                for r in range(LANES):
                    at = r * size + (2 * i + t) * most
                    outs[0][at : at + most, :] = rows[r * most : (r + 1) * most]

    return pick_call(body, sources, [LANES * size], after)[0]


def pick_onward(sources, planes, most, after=()):
    half = most // 2
    low = 2 * LANES * most

    def body(routes, refs, outs):
        for d in range(2):
            for t, rows in enumerate(pick(routes[d], planes[d][0], refs[d])):
                for r in range(LANES):
                    to = (2 * r + t) * most
                    outs[d][to : to + most, :] = rows[r * most : (r + 1) * most]
            for t, rows in enumerate(pick(routes[d], planes[d][1], refs[d])):
                for r in range(LANES):
                    to, at = low + (2 * r + t) * half, r * most + d * half
                    outs[d][to : to + half, :] = rows[at : at + half]

    return pick_call(body, sources, [low + low // 2] * 2, after)


def spread(up, down, rows, onward, after=()):
    width = up.shape[1]
    rest = up.shape[0] - rows
    size = rows // LANES

    def body(up_ref, down_ref, *refs):
        outs = refs[len(after) :]
        for r in range(LANES):
            for i, ref in enumerate((up_ref, down_ref)):
                to = (2 * r + i) * size
                outs[0][to : to + size, :] = ref[r * size : (r + 1) * size, :]
        if onward:
            outs[1][...] = up_ref[rows:, :]
            outs[2][...] = down_ref[rows:, :]

    shapes = [2 * rows] + [rest] * (2 * onward)

    def columns(count):
        return pl.BlockSpec((count, TILE), lambda i: (0, i))

    return pl.pallas_call(
        body,
        grid=(width // TILE,),
        out_shape=[jax.ShapeDtypeStruct((n, width), BF) for n in shapes],
        in_specs=[columns(up.shape[0])] * 2 + [ANYWHERE] * len(after),
        out_specs=[columns(n) for n in shapes],
        cost_estimate=LIGHT,
        compiler_params=PARAMS,
    )(up, down, *after)


def collect(back, place, lane_info, width):
    slots = back.shape[0]
    tok = place.shape[0]

    def body(info_ref, place_ref, back_ref, out_ref):
        slot = lax.broadcasted_iota(jnp.int32, (tok, slots), 1)
        most = 32
        expert = (slot // (4 * most)) * LANES + info_ref[0] * 2 + (slot // (2 * most)) % 2
        wanted = expert * most + slot % most
        wanted = jnp.where((slot // most) % 2 == info_ref[1], wanted, -1)
        hots = [place_ref[:, k : k + 1] == wanted for k in range(2)]
        hots = [h.astype(F32) for h in hots]
        both = (hots[0] + hots[1]).astype(BF)
        out_ref[:, :width] = dot(both, back_ref[:, :width]).astype(out_ref.dtype)
        tail = back_ref[:, width:]
        scores = [dot(h.astype(BF), tail) for h in hots]
        at = lax.broadcasted_iota(jnp.int32, scores[0].shape, 1)
        kept = jnp.where(at < 2, scores[0], jnp.where(at < 4, scores[1], 0.0))
        out_ref[:, width:] = kept.astype(out_ref.dtype)

    return pl.pallas_call(
        body,
        out_shape=jax.ShapeDtypeStruct((tok, back.shape[1]), BF),
        in_specs=[pl.BlockSpec(memory_space=pltpu.SMEM), WHOLE, WHOLE],
        out_specs=WHOLE,
        cost_estimate=LIGHT,
        compiler_params=PARAMS,
    )(jnp.stack(lane_info), place, back)


def chunk_grads(block, run, start, total_rows, places, shared, weights, after=()):
    rows, width = block.shape
    rows = rows // LANES
    size = rows // 2
    count = LANES * size
    ff = weights[0].shape[1]
    most = 32
    runs = size // run
    n_in = 2 + 3 + len(after) + len(shared)

    def body(*refs):
        place_ref = refs[0]
        gate_ref, up_ref, down_ref = refs[2:5]
        outs = refs[n_in : n_in + 5]
        x, g, hid, d, dx, wg, wu, wd, sems, out_sems = refs[n_in + 5 :]
        loads = [
            pltpu.make_async_copy(gate_ref, wg, sems.at[0]),
            pltpu.make_async_copy(up_ref, wu, sems.at[1]),
            pltpu.make_async_copy(down_ref, wd, sems.at[2]),
        ]
        pieces = []
        for t, into in enumerate((x, g)):
            for r in range(LANES):
                for i in range(runs):
                    pieces.append(
                        pltpu.make_async_copy(
                            refs[1].at[pl.ds(r * rows + (2 * i + t) * run, run), :],
                            into.at[pl.ds(r * size + i * run, run), :],
                            sems.at[3 + len(pieces)],
                        )
                    )
        split = len(pieces) // 2
        for copy in pieces[:split] + loads[:2] + pieces[split:] + loads[2:]:
            copy.start()
        stores = []

        def store(part, ref):
            stores.append(pltpu.make_async_copy(part, ref, out_sems.at[len(stores)]))
            stores[-1].start()

        mine = pl.ds(start, count)
        for copy in pieces[:split]:
            copy.wait()
        store(x, outs[0].at[mine, :])
        loads[0].wait()
        pre_gate = dot(x[...], wg[...])
        loads[1].wait()
        pre_up = dot(x[...], wu[...])
        sig = jax.nn.sigmoid(pre_gate)
        silu = pre_gate * sig
        hidden = silu * pre_up
        hid[...] = hidden.astype(BF)
        store(hid, outs[2].at[mine, :])
        for copy in pieces[split:]:
            copy.wait()
        store(g, outs[1].at[mine, :])
        loads[2].wait()
        grad_hidden = dot(g[...], wd[...], SECOND)
        score = jnp.sum(hid[...].astype(F32) * grad_hidden, axis=1, keepdims=True)
        high = score.astype(BF).astype(F32)
        at = lax.broadcasted_iota(jnp.int32, (count, SCORE), 1)
        tail = jnp.where(at % 2 == 0, high, score - high)
        dx[:, width:] = jnp.where(at < 4, tail, 0.0).astype(BF)
        d_gate = (grad_hidden * pre_up * sig * (1.0 + pre_gate * (1.0 - sig))).astype(BF)
        d_up = (grad_hidden * silu).astype(BF)
        d[:, :ff] = d_gate
        d[:, ff:] = d_up
        store(d, outs[3].at[mine, :])
        back = dot(d_gate, wg[...], SECOND) + dot(d_up, wu[...], SECOND)
        dx[:, :width] = back.astype(BF)
        for b in range(count // most):
            to = pl.multiple_of(place_ref[b], most)
            store(dx.at[pl.ds(b * most, most), :], outs[4].at[pl.ds(to, most), :])
        for copy in stores:
            copy.wait()

    shapes = [width, width, ff, 2 * ff, width + SCORE]
    first = 5 + len(after)
    return pl.pallas_call(
        body,
        out_shape=[jax.ShapeDtypeStruct((total_rows, n), BF) for n in shapes],
        in_specs=[pl.BlockSpec(memory_space=pltpu.SMEM)] + [ANYWHERE] * (n_in - 1),
        out_specs=[ANYWHERE] * 5,
        input_output_aliases={first + i: i for i in range(len(shared))},
        scratch_shapes=[
            pltpu.VMEM((count, width), BF),
            pltpu.VMEM((count, width), BF),
            pltpu.VMEM((count, ff), BF),
            pltpu.VMEM((count, 2 * ff), BF),
            pltpu.VMEM((count, width + SCORE), BF),
            pltpu.VMEM((width, ff), BF),
            pltpu.VMEM((width, ff), BF),
            pltpu.VMEM((ff, width), BF),
            pltpu.SemaphoreType.DMA((3 + 2 * LANES * runs,)),
            pltpu.SemaphoreType.DMA((4 + count // most,)),
        ],
        cost_estimate=LIGHT,
        compiler_params=PARAMS,
    )(places, block, *weights, *after, *shared)


def weight_grads(x, d, hidden, g):
    count, width = x.shape
    ff = hidden.shape[1]
    tile = 512

    def body(x_ref, d_ref, hidden_ref, g_ref, down_ref, in_ref):
        down_ref[...] = dot(hidden_ref[...], g_ref[...], FIRST).astype(BF)
        in_ref[...] = dot(x_ref[...], d_ref[...], FIRST).astype(BF)

    def fixed(a):
        return pl.BlockSpec(a.shape, lambda i: (0, 0))

    moving = pl.BlockSpec((count, tile), lambda i: (0, i))

    return pl.pallas_call(
        body,
        grid=(width // tile,),
        out_shape=[
            jax.ShapeDtypeStruct((ff, width), BF),
            jax.ShapeDtypeStruct((width, 2 * ff), BF),
        ],
        in_specs=[moving, fixed(d), fixed(hidden), moving],
        out_specs=[
            pl.BlockSpec((ff, tile), lambda i: (0, i)),
            pl.BlockSpec((tile, 2 * ff), lambda i: (i, 0)),
        ],
        cost_estimate=LIGHT,
        compiler_params=PARAMS,
    )(x, d, hidden, g)


def total(a, b, parts, after):
    rows, columns = a.shape
    tile, part = rows // 4, columns // parts

    def body(a_ref, b_ref, *refs):
        both = (a_ref[...].astype(F32) + b_ref[...].astype(F32)).astype(BF)
        for i in range(parts):
            refs[len(after) + i][...] = both[:, i * part : (i + 1) * part]

    def block(count):
        return pl.BlockSpec((tile, count), lambda i: (i, 0))

    return pl.pallas_call(
        body,
        grid=(4,),
        out_shape=[jax.ShapeDtypeStruct((rows, part), BF)] * parts,
        in_specs=[block(columns)] * 2 + [ANYWHERE] * len(after),
        out_specs=[block(part)] * parts,
        cost_estimate=LIGHT,
        compiler_params=PARAMS,
    )(a, b, *after)


def per_device(acts, grad_out, expert_of, slot_of, source_row, combine, w_gate, w_up, w_down):
    me = lax.axis_index("expert")
    z = me // LANES
    col = (me // 2) % 2
    tok = acts.shape[1]
    width = acts.shape[2]
    experts = source_row.shape[1]
    most = source_row.shape[2]
    sections = lax.axis_size("section")
    weight_gate = w_gate[0, 0]
    weight_up = w_up[0, 0]
    weight_down = w_down[0, 0]
    up_ring = ring_step(1)
    down_ring = ring_step(-1)

    place = expert_of[0] * most + (slot_of[0] - me * most)
    place_across = lax.ppermute(place, "expert", ACROSS)
    own = route_rows(
        acts[0], grad_out[0], source_row[0], expert_of[0].T, combine[0].T, me
    )
    plus1 = lax.ppermute(own, "expert", up_ring)
    minus1 = lax.ppermute(own, "expert", down_ring)
    plus2 = lax.ppermute(plus1, "expert", up_ring)
    minus2 = lax.ppermute(minus1, "expert", down_ring)

    def exchange(block):
        return lax.all_to_all(
            block, "expert", 0, 0, tiled=True, axis_index_groups=PLANE_GROUPS
        )

    slot_count = experts * most
    offsets_of = ((0,), (-1, 1), (-2, 2), (-3, 3), (4,))
    starts = [b * LANES * most for b in (0, 1, 3, 5, 7)]

    def places(offsets):
        found = []
        for other in range(LANES):
            for o in offsets:
                ring = (z + o + RING) % RING
                found.append(((ring * 2 + other % 2) * 2 + other // 2) * most)
        return jnp.stack(found).astype(jnp.int32)

    expert_weights = (weight_gate, weight_up, weight_down)

    def work(i, blocks, run, shared, after=()):
        return chunk_grads(
            blocks, run, starts[i], slot_count, places(offsets_of[i]), shared, expert_weights, after
        )

    own_out = pick_lanes([own], [0], most, after=[place_across])
    here_rows = exchange(own_out)
    shared = work(0, here_rows, most, [])
    near_out = pick_lanes([plus1, minus1], [1, RING - 1], most, after=[own_out])
    near = exchange(near_out)
    onward_up, onward_down = pick_onward(
        [plus2, minus2], [[3, 4], [RING - 3, RING - 4]], most, after=[near_out, shared[4]]
    )
    plus3 = lax.ppermute(onward_up, "expert", up_ring)
    minus3 = lax.ppermute(onward_down, "expert", down_ring)
    mid_out = pick_lanes([plus2, minus2], [2, RING - 2], most, after=[onward_up])
    mid = exchange(mid_out)
    shared = work(1, near, most, shared, after=[mid_out])
    far_out, last_up, last_down = spread(
        plus3, minus3, 2 * LANES * most, True, after=[shared[4]]
    )
    plus4 = lax.ppermute(last_up, "expert", up_ring)
    minus4 = lax.ppermute(last_down, "expert", down_ring)
    far = exchange(far_out)
    shared = work(2, mid, most, shared, after=[far_out])
    (last_out,) = spread(plus4, minus4, LANES * most, False, after=[shared[4]])
    last = exchange(last_out)
    shared = work(3, far, most, shared, after=[last_out])
    shared = work(4, last, most // 2, shared)

    x_all, g_all, hidden, d_rows, dx = shared
    down_part, in_parts = weight_grads(x_all, d_rows, hidden, g_all)
    mirror = [(s, sections - 1 - s) for s in range(sections)]
    down_far = lax.ppermute(down_part, "section", mirror)
    in_far = lax.ppermute(in_parts, "section", mirror)

    back = lax.all_to_all(
        dx.reshape(2 * RING, 2 * most, width + SCORE),
        "expert",
        0,
        0,
        tiled=True,
        axis_index_groups=COLUMN_GROUPS,
    ).reshape(-1, width + SCORE)
    leaving = collect(back, place_across, [col, 1 - col], width)
    away = lax.ppermute(leaving, "expert", ACROSS)
    here = collect(back, place, [col, col], width)
    both = here.astype(F32) + away.astype(F32)
    grad_acts = both[:, :width].astype(BF)
    found = jnp.stack([both[:, width + 2 * k] + both[:, width + 2 * k + 1] for k in range(2)], 1)
    grad_combine = (found / combine[0].astype(F32)).astype(BF)
    (grad_down,) = total(down_part, down_far, 1, [leaving])
    grad_gate, grad_up = total(in_parts, in_far, 2, [grad_down])
    return (
        grad_acts[None],
        grad_combine[None],
        grad_gate[None, None],
        grad_up[None, None],
        grad_down[None, None],
    )


def solution(mesh):
    return jax.shard_map(
        per_device,
        mesh=mesh,
        in_specs=(
            P("section", "expert", None),
            P("section", "expert", None),
            P("section", "expert", None),
            P("section", "expert", None),
            P("section", None, "expert"),
            P("section", "expert", None),
            P("section", "expert", None, None),
            P("section", "expert", None, None),
            P("section", "expert", None, None),
        ),
        out_specs=(
            P("section", "expert", None),
            P("section", "expert", None),
            P("section", "expert", None, None),
            P("section", "expert", None, None),
            P("section", "expert", None, None),
        ),
        check_vma=False,
    )
```

```python
import jax
import jax.numpy as jnp
from jax import lax
from jax.experimental import pallas as pl
from jax.experimental.pallas import tpu as pltpu
from jax.sharding import PartitionSpec as P

BF = jnp.bfloat16
F32 = jnp.float32
RING = 8
LANES = 4


def ring_step(step):
    return [
        (z * LANES + lane, ((z + step) % RING) * LANES + lane)
        for z in range(RING)
        for lane in range(LANES)
    ]


PLANE_GROUPS = [[z * LANES + lane for lane in range(LANES)] for z in range(RING)]
COLUMN_GROUPS = [
    [z * LANES + 2 * col + core for z in range(RING) for core in range(2)] for col in range(2)
]
ACROSS = [(e, e ^ 2) for e in range(RING * LANES)]
FIRST = (((0,), (0,)), ((), ()))
SECOND = (((1,), (1,)), ((), ()))


def dot(a, b, dims=(((1,), (0,)), ((), ()))):
    return lax.dot_general(a, b, dims, preferred_element_type=F32)


ROUTE_ROWS = 16
SCORE = 128
ANYWHERE = pl.BlockSpec(memory_space=pl.ANY)
WHOLE = pl.BlockSpec(memory_space=pltpu.VMEM)
LIGHT = pl.CostEstimate(flops=1, bytes_accessed=1, transcendentals=0)
PARAMS = pltpu.CompilerParams(vmem_limit_bytes=63 * 1024 * 1024)
TILE = 512


def route_rows(acts, grads, source_row, experts_of, combine, me):
    tok, width = acts.shape
    most = source_row.shape[1]
    slots = LANES * most
    behind = tok + ROUTE_ROWS

    def body(me_ref, acts_ref, grads_ref, source_ref, expert_ref, combine_ref, out_ref, table):
        own = me_ref[0]
        own_z = own // LANES
        out_ref[:tok, :] = acts_ref[...]
        out_ref[behind:, :] = grads_ref[...]
        index = lax.broadcasted_iota(jnp.int32, (tok, slots), 0)
        which = lax.broadcasted_iota(jnp.int32, (1, slots), 1) // most
        experts = expert_ref[...].astype(F32).astype(BF)
        for p in range(RING):
            plane = lax.rem(own_z + p, RING) * LANES
            for r in range(LANES):
                row = source_ref[pl.ds(plane + r, 1), :]
                row = jnp.where(row >= 0, row - own * tok, -1)
                table[p : p + 1, r * most : (r + 1) * most] = row.astype(F32)
            hot = index == table[p : p + 1, :].astype(jnp.int32)
            hot = hot.astype(F32).astype(BF)
            named = dot(experts, hot)
            value = dot(combine_ref[...], hot)
            expert = (plane + which).astype(F32)
            weight = jnp.where(named == expert, value, 0.0)
            table[RING + p : RING + p + 1, :] = weight[0:1] + weight[1:2]
        out_ref[tok:behind, :] = jnp.zeros((ROUTE_ROWS, width), BF)
        out_ref[tok:behind, :slots] = table[...].astype(BF)

    return pl.pallas_call(
        body,
        out_shape=jax.ShapeDtypeStruct((behind + tok, width), BF),
        in_specs=[pl.BlockSpec(memory_space=pltpu.SMEM)] + [WHOLE] * 5,
        out_specs=WHOLE,
        scratch_shapes=[pltpu.VMEM((ROUTE_ROWS, slots), F32)],
        cost_estimate=LIGHT,
        compiler_params=PARAMS,
    )(me.reshape(1), acts, grads, source_row, experts_of, combine)


def pick(route, plane, ref):
    tok = (ref.shape[0] - ROUTE_ROWS) // 2
    names = route[plane : plane + 1, :].astype(jnp.int32)
    index = lax.broadcasted_iota(jnp.int32, (tok, names.shape[1]), 0)
    hot = index == names
    weight = jnp.where(hot, route[RING + plane : RING + plane + 1, :], 0.0).astype(BF)
    x = dot(hot.astype(F32).astype(BF), ref[:tok, :], FIRST).astype(BF)
    return x, dot(weight, ref[tok + ROUTE_ROWS :, :], FIRST).astype(BF)


def pick_call(body, sources, out_rows, after):
    rows, width = sources[0].shape
    tok = (rows - ROUTE_ROWS) // 2
    count = len(sources)
    slots = LANES * 32

    def inner(*refs):
        routes = [r[:, :slots].astype(F32) for r in refs[:count]]
        body(routes, refs[count : 2 * count], refs[2 * count + len(after) :])

    def columns(size):
        return pl.BlockSpec((size, TILE), lambda i: (0, i))

    return pl.pallas_call(
        inner,
        grid=(width // TILE,),
        out_shape=[jax.ShapeDtypeStruct((n, width), BF) for n in out_rows],
        in_specs=[pl.BlockSpec((ROUTE_ROWS, TILE), lambda i: (tok // ROUTE_ROWS, 0))] * count
        + [columns(rows)] * count
        + [ANYWHERE] * len(after),
        out_specs=[columns(n) for n in out_rows],
        cost_estimate=LIGHT,
        compiler_params=PARAMS,
    )(*sources, *sources, *after)


def pick_lanes(sources, planes, most, after=()):
    size = len(sources) * 2 * most

    def body(routes, refs, outs):
        for i in range(len(sources)):
            for t, rows in enumerate(pick(routes[i], planes[i], refs[i])):
                for r in range(LANES):
                    at = r * size + (2 * i + t) * most
                    outs[0][at : at + most, :] = rows[r * most : (r + 1) * most]

    return pick_call(body, sources, [LANES * size], after)[0]


def pick_onward(sources, planes, most, after=()):
    def body(routes, refs, outs):
        for d in range(2):
            for t, rows in enumerate(pick(routes[d], planes[d], refs[d])):
                for r in range(LANES):
                    to = (2 * r + t) * most
                    outs[d][to : to + most, :] = rows[r * most : (r + 1) * most]

    return pick_call(body, sources, [2 * LANES * most] * 2, after)


def pick_mid(sources, planes, beyond, most, after=()):
    half = most // 2
    size = 6 * most

    def body(routes, refs, outs):
        for d in range(2):
            for t, rows in enumerate(pick(routes[d], planes[d], refs[d])):
                for r in range(LANES):
                    to = r * size + (2 * d + t) * most
                    outs[0][to : to + most, :] = rows[r * most : (r + 1) * most]
            for t, rows in enumerate(pick(routes[d], beyond[d], refs[d])):
                for r in range(LANES):
                    to, at = r * size + 4 * most + (2 * d + t) * half, r * most + d * half
                    outs[0][to : to + half, :] = rows[at : at + half]

    return pick_call(body, sources, [LANES * size], after)[0]


def beyond_rows(block, most):
    rows, width = block.shape
    size = rows // LANES

    def body(block_ref, *outs):
        for r in range(LANES):
            for d in range(2):
                low = r * size + size - (2 - d) * most
                outs[d][r * most : (r + 1) * most, :] = block_ref[low : low + most, :]

    def columns(count):
        return pl.BlockSpec((count, TILE), lambda i: (0, i))

    return pl.pallas_call(
        body,
        grid=(width // TILE,),
        out_shape=[jax.ShapeDtypeStruct((LANES * most, width), BF)] * 2,
        in_specs=[columns(rows)],
        out_specs=[columns(LANES * most)] * 2,
        cost_estimate=LIGHT,
        compiler_params=PARAMS,
    )(block)


def spread(up, down, after=()):
    rows, width = up.shape
    size = rows // LANES

    def body(up_ref, down_ref, *refs):
        for r in range(LANES):
            for i, ref in enumerate((up_ref, down_ref)):
                to = (2 * r + i) * size
                refs[-1][to : to + size, :] = ref[r * size : (r + 1) * size, :]

    def columns(count):
        return pl.BlockSpec((count, TILE), lambda i: (0, i))

    return pl.pallas_call(
        body,
        grid=(width // TILE,),
        out_shape=jax.ShapeDtypeStruct((2 * rows, width), BF),
        in_specs=[columns(rows)] * 2 + [ANYWHERE] * len(after),
        out_specs=columns(2 * rows),
        cost_estimate=LIGHT,
        compiler_params=PARAMS,
    )(up, down, *after)


def collect(back, place, lane_info, width):
    slots = back.shape[0]
    tok = place.shape[0]

    def body(info_ref, place_ref, back_ref, out_ref):
        slot = lax.broadcasted_iota(jnp.int32, (tok, slots), 1)
        most = 32
        expert = (slot // (4 * most)) * LANES + info_ref[0] * 2 + (slot // (2 * most)) % 2
        wanted = expert * most + slot % most
        wanted = jnp.where((slot // most) % 2 == info_ref[1], wanted, -1)
        hots = [place_ref[:, k : k + 1] == wanted for k in range(2)]
        hots = [h.astype(F32) for h in hots]
        both = (hots[0] + hots[1]).astype(BF)
        out_ref[:, :width] = dot(both, back_ref[:, :width]).astype(out_ref.dtype)
        tail = back_ref[:, width:]
        scores = [dot(h.astype(BF), tail) for h in hots]
        at = lax.broadcasted_iota(jnp.int32, scores[0].shape, 1)
        kept = jnp.where(at < 2, scores[0], jnp.where(at < 4, scores[1], 0.0))
        out_ref[:, width:] = kept.astype(out_ref.dtype)

    return pl.pallas_call(
        body,
        out_shape=jax.ShapeDtypeStruct((tok, back.shape[1]), BF),
        in_specs=[pl.BlockSpec(memory_space=pltpu.SMEM), WHOLE, WHOLE],
        out_specs=WHOLE,
        cost_estimate=LIGHT,
        compiler_params=PARAMS,
    )(jnp.stack(lane_info), place, back)


def chunk_grads(blocks, moves, count, start, total_rows, places, shared, weights, after=()):
    width = blocks[0].shape[1]
    ff = weights[0].shape[1]
    most = 32
    n_in = 1 + len(blocks) + 3 + len(after) + len(shared)
    moves = sorted(moves, key=lambda move: move[2])

    def body(*refs):
        place_ref = refs[0]
        gate_ref, up_ref, down_ref = refs[1 + len(blocks) : 4 + len(blocks)]
        outs = refs[n_in : n_in + 5]
        x, g, hid, d, dx, wg, wu, wd, sems, out_sems = refs[n_in + 5 :]
        loads = [
            pltpu.make_async_copy(gate_ref, wg, sems.at[0]),
            pltpu.make_async_copy(up_ref, wu, sems.at[1]),
            pltpu.make_async_copy(down_ref, wd, sems.at[2]),
        ]
        pieces = [
            pltpu.make_async_copy(
                refs[1 + b].at[pl.ds(at, size), :],
                (x, g)[t].at[pl.ds(to, size), :],
                sems.at[3 + i],
            )
            for i, (b, at, t, to, size) in enumerate(moves)
        ]
        split = len(pieces) // 2
        for copy in pieces[:split] + loads[:2] + pieces[split:] + loads[2:]:
            copy.start()
        stores = []

        def store(part, ref):
            stores.append(pltpu.make_async_copy(part, ref, out_sems.at[len(stores)]))
            stores[-1].start()

        mine = pl.ds(start, count)
        for copy in pieces[:split]:
            copy.wait()
        store(x, outs[0].at[mine, :])
        loads[0].wait()
        pre_gate = dot(x[...], wg[...])
        loads[1].wait()
        pre_up = dot(x[...], wu[...])
        sig = jax.nn.sigmoid(pre_gate)
        silu = pre_gate * sig
        hidden = silu * pre_up
        hid[...] = hidden.astype(BF)
        store(hid, outs[2].at[mine, :])
        for copy in pieces[split:]:
            copy.wait()
        store(g, outs[1].at[mine, :])
        loads[2].wait()
        grad_hidden = dot(g[...], wd[...], SECOND)
        score = jnp.sum(hid[...].astype(F32) * grad_hidden, axis=1, keepdims=True)
        high = score.astype(BF).astype(F32)
        at = lax.broadcasted_iota(jnp.int32, (count, SCORE), 1)
        tail = jnp.where(at % 2 == 0, high, score - high)
        dx[:, width:] = jnp.where(at < 4, tail, 0.0).astype(BF)
        d_gate = (grad_hidden * pre_up * sig * (1.0 + pre_gate * (1.0 - sig))).astype(BF)
        d_up = (grad_hidden * silu).astype(BF)
        d[:, :ff] = d_gate
        d[:, ff:] = d_up
        store(d, outs[3].at[mine, :])
        back = dot(d_gate, wg[...], SECOND) + dot(d_up, wu[...], SECOND)
        dx[:, :width] = back.astype(BF)
        for b in range(count // most):
            to = pl.multiple_of(place_ref[b], most)
            store(dx.at[pl.ds(b * most, most), :], outs[4].at[pl.ds(to, most), :])
        for copy in stores:
            copy.wait()

    shapes = [width, width, ff, 2 * ff, width + SCORE]
    first = 4 + len(blocks) + len(after)
    return pl.pallas_call(
        body,
        out_shape=[jax.ShapeDtypeStruct((total_rows, n), BF) for n in shapes],
        in_specs=[pl.BlockSpec(memory_space=pltpu.SMEM)] + [ANYWHERE] * (n_in - 1),
        out_specs=[ANYWHERE] * 5,
        input_output_aliases={first + i: i for i in range(len(shared))},
        scratch_shapes=[
            pltpu.VMEM((count, width), BF),
            pltpu.VMEM((count, width), BF),
            pltpu.VMEM((count, ff), BF),
            pltpu.VMEM((count, 2 * ff), BF),
            pltpu.VMEM((count, width + SCORE), BF),
            pltpu.VMEM((width, ff), BF),
            pltpu.VMEM((width, ff), BF),
            pltpu.VMEM((ff, width), BF),
            pltpu.SemaphoreType.DMA((3 + len(moves),)),
            pltpu.SemaphoreType.DMA((4 + count // most,)),
        ],
        cost_estimate=LIGHT,
        compiler_params=PARAMS,
    )(places, *blocks, *weights, *after, *shared)


def weight_grads(x, d, hidden, g):
    count, width = x.shape
    ff = hidden.shape[1]
    tile = 512

    def body(x_ref, d_ref, hidden_ref, g_ref, down_ref, in_ref):
        down_ref[...] = dot(hidden_ref[...], g_ref[...], FIRST).astype(BF)
        in_ref[...] = dot(x_ref[...], d_ref[...], FIRST).astype(BF)

    def fixed(a):
        return pl.BlockSpec(a.shape, lambda i: (0, 0))

    moving = pl.BlockSpec((count, tile), lambda i: (0, i))

    return pl.pallas_call(
        body,
        grid=(width // tile,),
        out_shape=[
            jax.ShapeDtypeStruct((ff, width), BF),
            jax.ShapeDtypeStruct((width, 2 * ff), BF),
        ],
        in_specs=[moving, fixed(d), fixed(hidden), moving],
        out_specs=[
            pl.BlockSpec((ff, tile), lambda i: (0, i)),
            pl.BlockSpec((tile, 2 * ff), lambda i: (i, 0)),
        ],
        cost_estimate=LIGHT,
        compiler_params=PARAMS,
    )(x, d, hidden, g)


def total(a, b, parts, after):
    rows, columns = a.shape
    tile, part = rows // 4, columns // parts

    def body(a_ref, b_ref, *refs):
        both = (a_ref[...].astype(F32) + b_ref[...].astype(F32)).astype(BF)
        for i in range(parts):
            refs[len(after) + i][...] = both[:, i * part : (i + 1) * part]

    def block(count):
        return pl.BlockSpec((tile, count), lambda i: (i, 0))

    return pl.pallas_call(
        body,
        grid=(4,),
        out_shape=[jax.ShapeDtypeStruct((rows, part), BF)] * parts,
        in_specs=[block(columns)] * 2 + [ANYWHERE] * len(after),
        out_specs=[block(part)] * parts,
        cost_estimate=LIGHT,
        compiler_params=PARAMS,
    )(a, b, *after)


def per_device(acts, grad_out, expert_of, slot_of, source_row, combine, w_gate, w_up, w_down):
    me = lax.axis_index("expert")
    z = me // LANES
    col = (me // 2) % 2
    tok = acts.shape[1]
    width = acts.shape[2]
    experts = source_row.shape[1]
    most = source_row.shape[2]
    sections = lax.axis_size("section")
    weight_gate = w_gate[0, 0]
    weight_up = w_up[0, 0]
    weight_down = w_down[0, 0]
    up_ring = ring_step(1)
    down_ring = ring_step(-1)

    place = expert_of[0] * most + (slot_of[0] - me * most)
    place_across = lax.ppermute(place, "expert", ACROSS)
    own = route_rows(
        acts[0], grad_out[0], source_row[0], expert_of[0].T, combine[0].T, me
    )
    plus1 = lax.ppermute(own, "expert", up_ring)
    minus1 = lax.ppermute(own, "expert", down_ring)
    plus2 = lax.ppermute(plus1, "expert", up_ring)
    minus2 = lax.ppermute(minus1, "expert", down_ring)

    def exchange(block):
        return lax.all_to_all(
            block, "expert", 0, 0, tiled=True, axis_index_groups=PLANE_GROUPS
        )

    slot_count = experts * most
    offsets_of = ((0,), (-1, 1), (-2, 2), (-3, 3, 4))
    starts = [b * LANES * most for b in (0, 1, 3, 5)]

    def places(offsets):
        found = []
        for other in range(LANES):
            for o in offsets:
                ring = (z + o + RING) % RING
                found.append(((ring * 2 + other % 2) * 2 + other // 2) * most)
        return jnp.stack(found).astype(jnp.int32)

    expert_weights = (weight_gate, weight_up, weight_down)

    half = most // 2

    def moves_of(stride, sources, per_lane):
        return [
            (0, r * stride + (2 * i + t) * most, t, (r * per_lane + i) * most, most)
            for r in range(LANES)
            for i in range(sources)
            for t in range(2)
        ]

    def work(i, blocks, moves, shared, after=()):
        count = LANES * most * len(offsets_of[i])
        return chunk_grads(
            blocks,
            moves,
            count,
            starts[i],
            slot_count,
            places(offsets_of[i]),
            shared,
            expert_weights,
            after,
        )

    own_out = pick_lanes([own], [0], most, after=[place_across])
    here_rows = exchange(own_out)
    shared = work(0, [here_rows], moves_of(2 * most, 1, 1), [])
    near_out = pick_lanes([plus1, minus1], [1, RING - 1], most, after=[own_out])
    near = exchange(near_out)
    mid_out = pick_mid(
        [plus2, minus2], [2, RING - 2], [4, RING - 4], most, after=[near_out, shared[4]]
    )
    onward_up, onward_down = pick_onward(
        [plus2, minus2], [3, RING - 3], most, after=[mid_out]
    )
    plus3 = lax.ppermute(onward_up, "expert", up_ring)
    minus3 = lax.ppermute(onward_down, "expert", down_ring)
    mid = exchange(mid_out)
    shared = work(1, [near], moves_of(4 * most, 2, 2), shared, after=[onward_up])
    last_up, last_down = beyond_rows(mid, most)
    plus4 = lax.ppermute(last_up, "expert", ring_step(2))
    minus4 = lax.ppermute(last_down, "expert", ring_step(-2))
    far_out = spread(plus3, minus3, after=[shared[4]])
    far = exchange(far_out)
    shared = work(2, [mid], moves_of(6 * most, 2, 2), shared, after=[far_out, last_up])
    last_moves = [
        (1 + d, r * most + t * half, t, (3 * r + 2) * most + d * half, half)
        for r in range(LANES)
        for d in range(2)
        for t in range(2)
    ]
    shared = work(3, [far, plus4, minus4], moves_of(4 * most, 2, 3) + last_moves, shared)

    x_all, g_all, hidden, d_rows, dx = shared
    down_part, in_parts = weight_grads(x_all, d_rows, hidden, g_all)
    mirror = [(s, sections - 1 - s) for s in range(sections)]
    down_far = lax.ppermute(down_part, "section", mirror)
    in_far = lax.ppermute(in_parts, "section", mirror)

    back = lax.all_to_all(
        dx.reshape(2 * RING, 2 * most, width + SCORE),
        "expert",
        0,
        0,
        tiled=True,
        axis_index_groups=COLUMN_GROUPS,
    ).reshape(-1, width + SCORE)
    leaving = collect(back, place_across, [col, 1 - col], width)
    away = lax.ppermute(leaving, "expert", ACROSS)
    here = collect(back, place, [col, col], width)
    both = here.astype(F32) + away.astype(F32)
    grad_acts = both[:, :width].astype(BF)
    found = jnp.stack([both[:, width + 2 * k] + both[:, width + 2 * k + 1] for k in range(2)], 1)
    grad_combine = (found / combine[0].astype(F32)).astype(BF)
    (grad_down,) = total(down_part, down_far, 1, [leaving])
    grad_gate, grad_up = total(in_parts, in_far, 2, [grad_down])
    return (
        grad_acts[None],
        grad_combine[None],
        grad_gate[None, None],
        grad_up[None, None],
        grad_down[None, None],
    )


def solution(mesh):
    return jax.shard_map(
        per_device,
        mesh=mesh,
        in_specs=(
            P("section", "expert", None),
            P("section", "expert", None),
            P("section", "expert", None),
            P("section", "expert", None),
            P("section", None, "expert"),
            P("section", "expert", None),
            P("section", "expert", None, None),
            P("section", "expert", None, None),
            P("section", "expert", None, None),
        ),
        out_specs=(
            P("section", "expert", None),
            P("section", "expert", None),
            P("section", "expert", None, None),
            P("section", "expert", None, None),
            P("section", "expert", None, None),
        ),
        check_vma=False,
    )
```

```python
import jax
import jax.numpy as jnp
from jax import lax
from jax.experimental import pallas as pl
from jax.experimental.pallas import tpu as pltpu
from jax.sharding import PartitionSpec as P

BF = jnp.bfloat16
F32 = jnp.float32
RING = 8
LANES = 4


def ring_step(step):
    return [
        (z * LANES + lane, ((z + step) % RING) * LANES + lane)
        for z in range(RING)
        for lane in range(LANES)
    ]


PLANE_GROUPS = [[z * LANES + lane for lane in range(LANES)] for z in range(RING)]
COLUMN_GROUPS = [
    [z * LANES + 2 * col + core for z in range(RING) for core in range(2)] for col in range(2)
]
ACROSS = [(e, e ^ 2) for e in range(RING * LANES)]
FIRST = (((0,), (0,)), ((), ()))
SECOND = (((1,), (1,)), ((), ()))


def dot(a, b, dims=(((1,), (0,)), ((), ()))):
    return lax.dot_general(a, b, dims, preferred_element_type=F32)


ROUTE_ROWS = 16
SCORE = 128
ANYWHERE = pl.BlockSpec(memory_space=pl.ANY)
WHOLE = pl.BlockSpec(memory_space=pltpu.VMEM)
LIGHT = pl.CostEstimate(flops=1, bytes_accessed=1, transcendentals=0)
PARAMS = pltpu.CompilerParams(vmem_limit_bytes=63 * 1024 * 1024)
TILE = 1024


def route_rows(acts, grads, source_row, experts_of, combine, me):
    tok, width = acts.shape
    most = source_row.shape[1]
    slots = LANES * most
    behind = tok + ROUTE_ROWS

    def body(me_ref, acts_ref, grads_ref, source_ref, expert_ref, combine_ref, out_ref, table):
        own = me_ref[0]
        own_z = own // LANES
        out_ref[:tok, :] = acts_ref[...]
        out_ref[behind:, :] = grads_ref[...]
        index = lax.broadcasted_iota(jnp.int32, (tok, slots), 0)
        which = lax.broadcasted_iota(jnp.int32, (1, slots), 1) // most
        experts = expert_ref[...].astype(F32).astype(BF)
        for p in range(RING):
            plane = lax.rem(own_z + p, RING) * LANES
            for r in range(LANES):
                row = source_ref[pl.ds(plane + r, 1), :]
                row = jnp.where(row >= 0, row - own * tok, -1)
                table[p : p + 1, r * most : (r + 1) * most] = row.astype(F32)
            hot = index == table[p : p + 1, :].astype(jnp.int32)
            hot = hot.astype(F32).astype(BF)
            named = dot(experts, hot)
            value = dot(combine_ref[...], hot)
            expert = (plane + which).astype(F32)
            weight = jnp.where(named == expert, value, 0.0)
            table[RING + p : RING + p + 1, :] = weight[0:1] + weight[1:2]
        out_ref[tok:behind, :] = jnp.zeros((ROUTE_ROWS, width), BF)
        out_ref[tok:behind, :slots] = table[...].astype(BF)

    return pl.pallas_call(
        body,
        out_shape=jax.ShapeDtypeStruct((behind + tok, width), BF),
        in_specs=[pl.BlockSpec(memory_space=pltpu.SMEM)] + [WHOLE] * 5,
        out_specs=WHOLE,
        scratch_shapes=[pltpu.VMEM((ROUTE_ROWS, slots), F32)],
        cost_estimate=LIGHT,
        compiler_params=PARAMS,
    )(me.reshape(1), acts, grads, source_row, experts_of, combine)


def pick(route, plane, ref):
    tok = (ref.shape[0] - ROUTE_ROWS) // 2
    names = route[plane : plane + 1, :].astype(jnp.int32)
    index = lax.broadcasted_iota(jnp.int32, (tok, names.shape[1]), 0)
    hot = index == names
    weight = jnp.where(hot, route[RING + plane : RING + plane + 1, :], 0.0).astype(BF)
    x = dot(hot.astype(F32).astype(BF), ref[:tok, :], FIRST).astype(BF)
    return x, dot(weight, ref[tok + ROUTE_ROWS :, :], FIRST).astype(BF)


def pick_call(body, sources, out_rows, after):
    rows, width = sources[0].shape
    tok = (rows - ROUTE_ROWS) // 2
    count = len(sources)
    slots = LANES * 32

    def inner(*refs):
        routes = [r[:, :slots].astype(F32) for r in refs[:count]]
        body(routes, refs[count : 2 * count], refs[2 * count + len(after) :])

    def columns(size):
        return pl.BlockSpec((size, TILE), lambda i: (0, i))

    return pl.pallas_call(
        inner,
        grid=(width // TILE,),
        out_shape=[jax.ShapeDtypeStruct((n, width), BF) for n in out_rows],
        in_specs=[pl.BlockSpec((ROUTE_ROWS, TILE), lambda i: (tok // ROUTE_ROWS, 0))] * count
        + [columns(rows)] * count
        + [ANYWHERE] * len(after),
        out_specs=[columns(n) for n in out_rows],
        cost_estimate=LIGHT,
        compiler_params=PARAMS,
    )(*sources, *sources, *after)


def pick_lanes(sources, planes, most, after=()):
    size = len(sources) * 2 * most

    def body(routes, refs, outs):
        for i in range(len(sources)):
            for t, rows in enumerate(pick(routes[i], planes[i], refs[i])):
                for r in range(LANES):
                    at = r * size + (2 * i + t) * most
                    outs[0][at : at + most, :] = rows[r * most : (r + 1) * most]

    return pick_call(body, sources, [LANES * size], after)[0]


def pick_onward(sources, planes, most, after=()):
    def body(routes, refs, outs):
        for d in range(2):
            for t, rows in enumerate(pick(routes[d], planes[d], refs[d])):
                for r in range(LANES):
                    to = (2 * r + t) * most
                    outs[d][to : to + most, :] = rows[r * most : (r + 1) * most]

    return pick_call(body, sources, [2 * LANES * most] * 2, after)


def pick_mid(sources, planes, beyond, most, after=()):
    half = most // 2
    size = 6 * most

    def body(routes, refs, outs):
        for d in range(2):
            for t, rows in enumerate(pick(routes[d], planes[d], refs[d])):
                for r in range(LANES):
                    to = r * size + (2 * d + t) * most
                    outs[0][to : to + most, :] = rows[r * most : (r + 1) * most]
            for t, rows in enumerate(pick(routes[d], beyond[d], refs[d])):
                for r in range(LANES):
                    to, at = r * size + 4 * most + (2 * d + t) * half, r * most + d * half
                    outs[0][to : to + half, :] = rows[at : at + half]

    return pick_call(body, sources, [LANES * size], after)[0]


def beyond_rows(block, most):
    rows, width = block.shape
    size = rows // LANES

    def body(block_ref, *outs):
        for r in range(LANES):
            for d in range(2):
                low = r * size + size - (2 - d) * most
                outs[d][r * most : (r + 1) * most, :] = block_ref[low : low + most, :]

    def columns(count):
        return pl.BlockSpec((count, TILE), lambda i: (0, i))

    return pl.pallas_call(
        body,
        grid=(width // TILE,),
        out_shape=[jax.ShapeDtypeStruct((LANES * most, width), BF)] * 2,
        in_specs=[columns(rows)],
        out_specs=[columns(LANES * most)] * 2,
        cost_estimate=LIGHT,
        compiler_params=PARAMS,
    )(block)


def spread(up, down, after=()):
    rows, width = up.shape
    size = rows // LANES

    def body(up_ref, down_ref, *refs):
        for r in range(LANES):
            for i, ref in enumerate((up_ref, down_ref)):
                to = (2 * r + i) * size
                refs[-1][to : to + size, :] = ref[r * size : (r + 1) * size, :]

    def columns(count):
        return pl.BlockSpec((count, TILE), lambda i: (0, i))

    return pl.pallas_call(
        body,
        grid=(width // TILE,),
        out_shape=jax.ShapeDtypeStruct((2 * rows, width), BF),
        in_specs=[columns(rows)] * 2 + [ANYWHERE] * len(after),
        out_specs=columns(2 * rows),
        cost_estimate=LIGHT,
        compiler_params=PARAMS,
    )(up, down, *after)


def collect(back, place, lane_info, width):
    slots = back.shape[0]
    tok = place.shape[0]

    def body(info_ref, place_ref, back_ref, out_ref):
        slot = lax.broadcasted_iota(jnp.int32, (tok, slots), 1)
        most = 32
        expert = (slot // (4 * most)) * LANES + info_ref[0] * 2 + (slot // (2 * most)) % 2
        wanted = expert * most + slot % most
        wanted = jnp.where((slot // most) % 2 == info_ref[1], wanted, -1)
        hots = [place_ref[:, k : k + 1] == wanted for k in range(2)]
        hots = [h.astype(F32) for h in hots]
        both = (hots[0] + hots[1]).astype(BF)
        out_ref[:, :width] = dot(both, back_ref[:, :width]).astype(out_ref.dtype)
        tail = back_ref[:, width:]
        scores = [dot(h.astype(BF), tail) for h in hots]
        at = lax.broadcasted_iota(jnp.int32, scores[0].shape, 1)
        kept = jnp.where(at < 2, scores[0], jnp.where(at < 4, scores[1], 0.0))
        out_ref[:, width:] = kept.astype(out_ref.dtype)

    return pl.pallas_call(
        body,
        out_shape=jax.ShapeDtypeStruct((tok, back.shape[1]), BF),
        in_specs=[pl.BlockSpec(memory_space=pltpu.SMEM), WHOLE, WHOLE],
        out_specs=WHOLE,
        cost_estimate=LIGHT,
        compiler_params=PARAMS,
    )(jnp.stack(lane_info), place, back)


def chunk_grads(blocks, moves, count, start, total_rows, places, shared, weights, after=()):
    width = blocks[0].shape[1]
    ff = weights[0].shape[1]
    most = 32
    n_in = 1 + len(blocks) + 3 + len(after) + len(shared)
    moves = sorted(moves, key=lambda move: move[2])

    def body(*refs):
        place_ref = refs[0]
        gate_ref, up_ref, down_ref = refs[1 + len(blocks) : 4 + len(blocks)]
        outs = refs[n_in : n_in + 5]
        x, g, hid, d, dx, wg, wu, wd, sems, out_sems = refs[n_in + 5 :]
        loads = [
            pltpu.make_async_copy(gate_ref, wg, sems.at[0]),
            pltpu.make_async_copy(up_ref, wu, sems.at[1]),
            pltpu.make_async_copy(down_ref, wd, sems.at[2]),
        ]
        pieces = [
            pltpu.make_async_copy(
                refs[1 + b].at[pl.ds(at, size), :],
                (x, g)[t].at[pl.ds(to, size), :],
                sems.at[3 + i],
            )
            for i, (b, at, t, to, size) in enumerate(moves)
        ]
        split = len(pieces) // 2
        for copy in pieces[:split] + loads[:2] + pieces[split:] + loads[2:]:
            copy.start()
        stores = []

        def store(part, ref):
            stores.append(pltpu.make_async_copy(part, ref, out_sems.at[len(stores)]))
            stores[-1].start()

        mine = pl.ds(start, count)
        for copy in pieces[:split]:
            copy.wait()
        store(x, outs[0].at[mine, :])
        loads[0].wait()
        pre_gate = dot(x[...], wg[...])
        loads[1].wait()
        pre_up = dot(x[...], wu[...])
        sig = jax.nn.sigmoid(pre_gate)
        silu = pre_gate * sig
        hidden = silu * pre_up
        hid[...] = hidden.astype(BF)
        store(hid, outs[2].at[mine, :])
        for copy in pieces[split:]:
            copy.wait()
        store(g, outs[1].at[mine, :])
        loads[2].wait()
        grad_hidden = dot(g[...], wd[...], SECOND)
        score = jnp.sum(hid[...].astype(F32) * grad_hidden, axis=1, keepdims=True)
        high = score.astype(BF).astype(F32)
        at = lax.broadcasted_iota(jnp.int32, (count, SCORE), 1)
        tail = jnp.where(at % 2 == 0, high, score - high)
        dx[:, width:] = jnp.where(at < 4, tail, 0.0).astype(BF)
        d_gate = (grad_hidden * pre_up * sig * (1.0 + pre_gate * (1.0 - sig))).astype(BF)
        d_up = (grad_hidden * silu).astype(BF)
        d[:, :ff] = d_gate
        d[:, ff:] = d_up
        store(d, outs[3].at[mine, :])
        back = dot(d_gate, wg[...], SECOND) + dot(d_up, wu[...], SECOND)
        dx[:, :width] = back.astype(BF)
        for b in range(count // most):
            to = pl.multiple_of(place_ref[b], most)
            store(dx.at[pl.ds(b * most, most), :], outs[4].at[pl.ds(to, most), :])
        for copy in stores:
            copy.wait()

    shapes = [width, width, ff, 2 * ff, width + SCORE]
    first = 4 + len(blocks) + len(after)
    return pl.pallas_call(
        body,
        out_shape=[jax.ShapeDtypeStruct((total_rows, n), BF) for n in shapes],
        in_specs=[pl.BlockSpec(memory_space=pltpu.SMEM)] + [ANYWHERE] * (n_in - 1),
        out_specs=[ANYWHERE] * 5,
        input_output_aliases={first + i: i for i in range(len(shared))},
        scratch_shapes=[
            pltpu.VMEM((count, width), BF),
            pltpu.VMEM((count, width), BF),
            pltpu.VMEM((count, ff), BF),
            pltpu.VMEM((count, 2 * ff), BF),
            pltpu.VMEM((count, width + SCORE), BF),
            pltpu.VMEM((width, ff), BF),
            pltpu.VMEM((width, ff), BF),
            pltpu.VMEM((ff, width), BF),
            pltpu.SemaphoreType.DMA((3 + len(moves),)),
            pltpu.SemaphoreType.DMA((4 + count // most,)),
        ],
        cost_estimate=LIGHT,
        compiler_params=PARAMS,
    )(places, *blocks, *weights, *after, *shared)


def weight_grads(x, d, hidden, g):
    count, width = x.shape
    ff = hidden.shape[1]
    tile = 512

    def body(x_ref, d_ref, hidden_ref, g_ref, down_ref, in_ref):
        down_ref[...] = dot(hidden_ref[...], g_ref[...], FIRST).astype(BF)
        in_ref[...] = dot(x_ref[...], d_ref[...], FIRST).astype(BF)

    def fixed(a):
        return pl.BlockSpec(a.shape, lambda i: (0, 0))

    moving = pl.BlockSpec((count, tile), lambda i: (0, i))

    return pl.pallas_call(
        body,
        grid=(width // tile,),
        out_shape=[
            jax.ShapeDtypeStruct((ff, width), BF),
            jax.ShapeDtypeStruct((width, 2 * ff), BF),
        ],
        in_specs=[moving, fixed(d), fixed(hidden), moving],
        out_specs=[
            pl.BlockSpec((ff, tile), lambda i: (0, i)),
            pl.BlockSpec((tile, 2 * ff), lambda i: (i, 0)),
        ],
        cost_estimate=LIGHT,
        compiler_params=PARAMS,
    )(x, d, hidden, g)


def total(a, b, parts, after):
    rows, columns = a.shape
    tile, part = rows // 4, columns // parts

    def body(a_ref, b_ref, *refs):
        both = (a_ref[...].astype(F32) + b_ref[...].astype(F32)).astype(BF)
        for i in range(parts):
            refs[len(after) + i][...] = both[:, i * part : (i + 1) * part]

    def block(count):
        return pl.BlockSpec((tile, count), lambda i: (i, 0))

    return pl.pallas_call(
        body,
        grid=(4,),
        out_shape=[jax.ShapeDtypeStruct((rows, part), BF)] * parts,
        in_specs=[block(columns)] * 2 + [ANYWHERE] * len(after),
        out_specs=[block(part)] * parts,
        cost_estimate=LIGHT,
        compiler_params=PARAMS,
    )(a, b, *after)


def per_device(acts, grad_out, expert_of, slot_of, source_row, combine, w_gate, w_up, w_down):
    me = lax.axis_index("expert")
    z = me // LANES
    col = (me // 2) % 2
    tok = acts.shape[1]
    width = acts.shape[2]
    experts = source_row.shape[1]
    most = source_row.shape[2]
    sections = lax.axis_size("section")
    weight_gate = w_gate[0, 0]
    weight_up = w_up[0, 0]
    weight_down = w_down[0, 0]
    up_ring = ring_step(1)
    down_ring = ring_step(-1)

    place = expert_of[0] * most + (slot_of[0] - me * most)
    place_across = lax.ppermute(place, "expert", ACROSS)
    own = route_rows(
        acts[0], grad_out[0], source_row[0], expert_of[0].T, combine[0].T, me
    )
    plus1 = lax.ppermute(own, "expert", up_ring)
    minus1 = lax.ppermute(own, "expert", down_ring)
    plus2 = lax.ppermute(plus1, "expert", up_ring)
    minus2 = lax.ppermute(minus1, "expert", down_ring)

    def exchange(block):
        return lax.all_to_all(
            block, "expert", 0, 0, tiled=True, axis_index_groups=PLANE_GROUPS
        )

    slot_count = experts * most
    offsets_of = ((0,), (-1, 1), (-2, 2), (-3, 3, 4))
    starts = [b * LANES * most for b in (0, 1, 3, 5)]

    def places(offsets):
        found = []
        for other in range(LANES):
            for o in offsets:
                ring = (z + o + RING) % RING
                found.append(((ring * 2 + other % 2) * 2 + other // 2) * most)
        return jnp.stack(found).astype(jnp.int32)

    expert_weights = (weight_gate, weight_up, weight_down)

    half = most // 2

    def moves_of(stride, sources, per_lane):
        return [
            (0, r * stride + (2 * i + t) * most, t, (r * per_lane + i) * most, most)
            for r in range(LANES)
            for i in range(sources)
            for t in range(2)
        ]

    def work(i, blocks, moves, shared, after=()):
        count = LANES * most * len(offsets_of[i])
        return chunk_grads(
            blocks,
            moves,
            count,
            starts[i],
            slot_count,
            places(offsets_of[i]),
            shared,
            expert_weights,
            after,
        )

    own_out = pick_lanes([own], [0], most, after=[place_across])
    here_rows = exchange(own_out)
    shared = work(0, [here_rows], moves_of(2 * most, 1, 1), [])
    near_out = pick_lanes([plus1, minus1], [1, RING - 1], most, after=[own_out])
    near = exchange(near_out)
    mid_out = pick_mid(
        [plus2, minus2], [2, RING - 2], [4, RING - 4], most, after=[near_out, shared[4]]
    )
    onward_up, onward_down = pick_onward(
        [plus2, minus2], [3, RING - 3], most, after=[mid_out]
    )
    plus3 = lax.ppermute(onward_up, "expert", up_ring)
    minus3 = lax.ppermute(onward_down, "expert", down_ring)
    mid = exchange(mid_out)
    shared = work(1, [near], moves_of(4 * most, 2, 2), shared, after=[onward_up])
    last_up, last_down = beyond_rows(mid, most)
    plus4 = lax.ppermute(last_up, "expert", ring_step(2))
    minus4 = lax.ppermute(last_down, "expert", ring_step(-2))
    far_out = spread(plus3, minus3, after=[shared[4]])
    far = exchange(far_out)
    shared = work(2, [mid], moves_of(6 * most, 2, 2), shared, after=[far_out, last_up])
    last_moves = [
        (1 + d, r * most + t * half, t, (3 * r + 2) * most + d * half, half)
        for r in range(LANES)
        for d in range(2)
        for t in range(2)
    ]
    shared = work(3, [far, plus4, minus4], moves_of(4 * most, 2, 3) + last_moves, shared)

    x_all, g_all, hidden, d_rows, dx = shared
    down_part, in_parts = weight_grads(x_all, d_rows, hidden, g_all)
    mirror = [(s, sections - 1 - s) for s in range(sections)]
    down_far = lax.ppermute(down_part, "section", mirror)
    in_far = lax.ppermute(in_parts, "section", mirror)

    back = lax.all_to_all(
        dx.reshape(2 * RING, 2 * most, width + SCORE),
        "expert",
        0,
        0,
        tiled=True,
        axis_index_groups=COLUMN_GROUPS,
    ).reshape(-1, width + SCORE)
    leaving = collect(back, place_across, [col, 1 - col], width)
    away = lax.ppermute(leaving, "expert", ACROSS)
    here = collect(back, place, [col, col], width)
    both = here.astype(F32) + away.astype(F32)
    grad_acts = both[:, :width].astype(BF)
    found = jnp.stack([both[:, width + 2 * k] + both[:, width + 2 * k + 1] for k in range(2)], 1)
    grad_combine = (found / combine[0].astype(F32)).astype(BF)
    (grad_down,) = total(down_part, down_far, 1, [leaving])
    grad_gate, grad_up = total(in_parts, in_far, 2, [grad_down])
    return (
        grad_acts[None],
        grad_combine[None],
        grad_gate[None, None],
        grad_up[None, None],
        grad_down[None, None],
    )


def solution(mesh):
    return jax.shard_map(
        per_device,
        mesh=mesh,
        in_specs=(
            P("section", "expert", None),
            P("section", "expert", None),
            P("section", "expert", None),
            P("section", "expert", None),
            P("section", None, "expert"),
            P("section", "expert", None),
            P("section", "expert", None, None),
            P("section", "expert", None, None),
            P("section", "expert", None, None),
        ),
        out_specs=(
            P("section", "expert", None),
            P("section", "expert", None),
            P("section", "expert", None, None),
            P("section", "expert", None, None),
            P("section", "expert", None, None),
        ),
        check_vma=False,
    )
```
